256 devices in a mesh: gx: 16 (over y_lo, z), gz: 8 (over x, y_hi), gy: 2 (over core).
Axes of the slice: x: 4, y: 4 (y_hi: 2, y_lo: 2; y = y_hi * 2 + y_lo), z: 8, core: 2. Of those that a mesh axis runs over, the one named last changes fastest.
Arguments:
- field: bfloat16 [8, 384, 384, 256], P(None, 'gx', 'gz', 'gy'), may hold values from -25 to 25
- x_factor: bfloat16 [384, 48], P('gx'), may hold values from -0.3125 to 0.3125
- y_factor: bfloat16 [256, 48], P('gy'), may hold values from -0.375 to 0.375
- species_basis_matrix: float32 [8, 4], replicated, may hold values from -2 to 2
Outputs:
- gram: float32 [384, 384], P('gz')
The draws below stay inside these ranges and needn't reach their ends.
All inputs are finite; a program needn't handle non-finite values.
Results may differ from the reference program's by a relative error of at most 0.0003.
Values may be sent and summed in bfloat16 or wider, within the bound.
A program may use at most 64 MiB of HBM per device.

```python
import math
import jax
import jax.numpy as jnp
from jax import lax

NS = 8
RX = 48
RY = 48
RS = 4
NX = 384
NY = 256
NZ = 384


def draw_field(key, part):
    key = jax.random.fold_in(key, 11)
    first, second, third = jax.random.split(key, 3)
    species_magnitude = jnp.exp(jax.random.uniform(first, (NS, 1, 1, 1), jnp.float32, math.log(0.7), math.log(1.4)))
    plane_magnitude = jnp.exp(jax.random.uniform(second, (1, 1, NZ, 1), jnp.float32, math.log(0.5), math.log(1.6)))
    values = jnp.clip(jax.random.normal(third, (NS, NX, NZ, NY), jnp.float32), -4.0, 4.0)
    return (species_magnitude * plane_magnitude * values).astype(jnp.bfloat16)


def block_scale(own_key, dims, pieces, smallest, largest):
    def one(axis_at, shards_of):
        heights = jax.random.uniform(jax.random.fold_in(jax.random.fold_in(own_key, 6), axis_at), (shards_of,), jnp.float32, smallest / len(pieces), largest / len(pieces))
        return jnp.repeat(jnp.exp(heights), dims[axis_at] // shards_of).reshape((-1,) + (1,) * (len(dims) - axis_at - 1))

    factor_of = one(*pieces[0])
    for cut in pieces[1:]:
        factor_of = factor_of * one(*cut)
    return factor_of


def gaussian(key, extent, deviation, reach, cuts=(), held_as=jnp.bfloat16):
    entries = deviation * jax.random.normal(key, extent, jnp.float32)
    if cuts:
        entries = entries * block_scale(key, extent, cuts, -0.22, 0.18)
    return jnp.clip(entries, -reach, reach).astype(held_as)


def setup_inputs(seed: int = 0) -> dict:
    seeds = jax.random.split(jax.random.key(seed), 5)
    field = draw_field(jax.random.fold_in(seeds[4], 71), 0)
    x_factor = gaussian(seeds[1], (NX, RX), NX ** -0.5, 0.3125, ((0, 16),))
    y_factor = gaussian(seeds[2], (NY, RY), NY ** -0.5, 0.375, ((0, 2),))
    species_basis_matrix = gaussian(seeds[3], (NS, RS), NS ** -0.5, 2.0, (), jnp.float32)
    return {"field": field, "x_factor": x_factor, "y_factor": y_factor, "species_basis_matrix": species_basis_matrix}


def reference(field, x_factor, y_factor, species_basis_matrix):
    def project(slab):
        flat = slab.reshape(-1, slab.shape[-1])
        product = jnp.dot(flat, y_factor, preferred_element_type=jnp.float32)
        return product.reshape(slab.shape[0], slab.shape[1], -1)

    across_y_axis = lax.map(project, field)
    reduced_tensor = jnp.einsum("sxzj,sp->pxzj", across_y_axis, species_basis_matrix.astype(jnp.float32), precision=lax.Precision.HIGHEST)
    core = jnp.einsum("xi,pxzj->zpji", x_factor.astype(jnp.float32), reduced_tensor, precision=lax.Precision.HIGHEST)
    unfolded = core.reshape(core.shape[0], -1)
    products = jnp.dot(unfolded, unfolded.T, precision=lax.Precision.HIGHEST)
    return products / (RX * RY * RS)
```

```python
import functools

import jax
import jax.numpy as jnp
from jax import lax
from jax.experimental import pallas as pl
from jax.experimental.pallas import tpu as pltpu
from jax.sharding import PartitionSpec as P

MESH = pl.DeviceIdType.MESH
F32 = jnp.float32
BF16 = jnp.bfloat16
NT = (((1,), (1,)), ((), ()))

NGX, NGZ, NGY = 16, 8, 2
XL, ZL = 24, 48
RI, RJ, RP, NS = 48, 48, 4, 8
ZG, ZZ = 10, 5
TOP = 32000.0
BIAS = 124.0
SHARE = 6
CH = 4
ROWS = XL * ZL // CH


def encode(value, inverse):
    whole = jnp.round(value * inverse)
    size = jnp.abs(whole)
    high = jnp.floor(size * (1.0 / 128.0))
    code = jnp.exp2(high - BIAS) * (1.0 + (size - 128.0 * high) * (1.0 / 128.0))
    return jnp.where(whole < 0.0, -code, code)


def decode(code):
    size = jnp.abs(code)
    high = jnp.floor(jnp.log2(size) + 0.002)
    whole = jnp.round(128.0 * (high + (BIAS - 1.0) + size * jnp.exp2(-high)))
    return jnp.where(code < 0.0, -whole, whole)


def scale_of(largest):
    unit = (largest * (1.01 / TOP)).astype(BF16).astype(F32)
    return jnp.maximum(unit, 2.0**-100)


def split(value):
    high = value.astype(BF16)
    return high, (value - high.astype(F32)).astype(BF16)


def kernel(field, xf, yf, sb, out, fbuf, whi, wlo, mine, other, prt, tsum, xsend, xrecv, bd, asend, arecv, acc, d2,
           cbuf, chi, clo, gpart, rrecv, red, ofull,
           f_sem, es_sem, er_sem, xs_sem, xr_sem, as_sem, ar_sem, cs_sem, cr_sem, rs_sem, rr_sem, bs_sem, br_sem):
    gx, gz, gy = lax.axis_index("gx"), lax.axis_index("gz"), lax.axis_index("gy")
    line = gx * 2 + gy

    def to_gx(dd):
        return {"gx": (gx + dd) % NGX, "gz": gz, "gy": gy}

    def to_gz(e):
        return {"gx": gx, "gz": (gz + e) % NGZ, "gy": gy}

    def to_line(k):
        there = (line + k) % 32
        return {"gx": there // 2, "gz": gz, "gy": there % 2}

    loads = []
    for c in range(CH):
        part = pl.ds(c * (XL // CH), XL // CH)
        loads.append(pltpu.make_async_copy(field.at[:, part], fbuf.at[:, part], f_sem.at[c]))
        loads[-1].start()

    barrier = pltpu.get_barrier_semaphore()

    def greet(k, _):
        pl.semaphore_signal(barrier, inc=1, device_id=to_line(k), device_id_type=MESH)
        return 0

    lax.fori_loop(1, 32, greet, 0)
    for e in range(1, NGZ):
        pl.semaphore_signal(barrier, inc=1, device_id=to_gz(e), device_id_type=MESH)

    x32 = xf[...].astype(F32)
    low = jnp.concatenate([x32[16:24], jnp.zeros((8, RI), F32)], axis=0)
    gap = jnp.zeros((16, 16), F32)
    xsend[...] = jnp.concatenate([x32[0:16], gap, low, gap], axis=1).astype(BF16)

    lane = lax.broadcasted_iota(jnp.int32, (RJ, 256), 1)
    q = lane & 7
    dest = (gx + ((lane >> 3) & 15)) & 15
    late = (q >= 3).astype(jnp.int32)
    jl = 3 * dest + q - 3 * late
    pick = (lax.broadcasted_iota(jnp.int32, (RJ, 256), 0) == jl) & (q < SHARE)
    spread = jnp.dot(yf[...], pick.astype(F32).astype(BF16), preferred_element_type=F32)
    plane = (2 * (((lane >> 7) + gy) & 1) + late)[0:NS]
    basis = sb[...]
    mix = jnp.zeros((NS, 256), F32)
    for p in range(RP):
        mix = mix + jnp.where(plane == p, basis[:, p:p + 1], 0.0)
    for s in range(NS):
        high, rest = split(spread * mix[s:s + 1, :])
        whi[128 * s:128 * s + 128, :] = high
        wlo[128 * s:128 * s + 128, :] = rest

    pl.semaphore_wait(barrier, 31 + NGZ - 1)

    xcopies = [
        pltpu.make_async_remote_copy(xsend, xrecv.at[dd], xs_sem.at[dd], xr_sem.at[dd], device_id=to_gx(dd), device_id_type=MESH)
        for dd in range(1, NGX)
    ]
    for copy in xcopies:
        copy.start()

    exchanges = []
    for c in range(CH):
        loads[c].wait()
        left = jnp.concatenate(
            [fbuf[s, c * (XL // CH):(c + 1) * (XL // CH)].reshape(ROWS, 128) for s in range(NS)], axis=1)
        part = jnp.dot(left, whi[...], preferred_element_type=F32) + jnp.dot(left, wlo[...], preferred_element_type=F32)
        span = pl.ds(c * ROWS, ROWS)
        mine[span, :] = part[:, 0:128]
        other[span, :] = part[:, 128:256]
        exchanges.append(pltpu.make_async_remote_copy(
            other.at[span], prt.at[span], es_sem.at[c], er_sem.at[c],
            device_id={"gx": gx, "gz": gz, "gy": 1 - gy}, device_id_type=MESH))
        exchanges[-1].start()

    largest = jnp.zeros((8, 128), F32)
    for c in range(CH):
        exchanges[c].wait_recv()
        span = pl.ds(c * ROWS, ROWS)
        total = mine[span, :] + prt[span, :]
        tsum[span, :] = total
        largest = jnp.maximum(largest, jnp.max(jnp.abs(total).reshape(ROWS // 8, 8, 128), axis=0))
    unit = scale_of(jnp.max(largest, keepdims=True))
    inverse = 1.0 / unit

    is_scale = lax.broadcasted_iota(jnp.int32, (NGX, 8, 128), 1) == SHARE

    def coded(zg):
        pieces = []
        for zz in range(ZZ):
            z = zg + ZG * zz
            pieces.append(tsum[pl.ds(z, XL, stride=ZL), :] if z < ZL else jnp.zeros((XL, 128), F32))
        pieces.append(jnp.zeros((8, 128), F32))
        tile = jnp.concatenate(pieces, axis=0).T
        return jnp.where(is_scale, unit.reshape(1, 1, 1), encode(tile, inverse).reshape(NGX, 8, 128))

    for m in range(ZG // 2):
        both = jnp.concatenate([coded(2 * m), coded(2 * m + 1)], axis=1)
        asend[:, 16 * m:16 * m + 16, :] = both.astype(BF16)

    acopies = {
        dd: pltpu.make_async_remote_copy(asend.at[dd], arecv.at[dd], as_sem.at[dd], ar_sem.at[dd], device_id=to_gx(dd), device_id_type=MESH)
        for dd in range(1, NGX)
    }
    for dd in range(1, NGX):
        acopies[dd].start()

    for copy in xcopies:
        copy.wait_recv()
    xrecv[0] = xsend[...]
    row = lax.broadcasted_iota(jnp.int32, (128, 256), 0)
    lane = lax.broadcasted_iota(jnp.int32, (128, 256), 1)
    slot = jnp.zeros((128, 256), jnp.int32)
    for zz in range(1, ZZ):
        slot = slot + (lane >= RI * zz).astype(jnp.int32)
    want = lane - RI * slot
    first = ((row == want) & (lane < RI * ZZ)).astype(F32).astype(BF16)
    second = ((row == want + 64) & (lane < RI * ZZ)).astype(F32).astype(BF16)
    everything = xrecv[...].reshape(NGX * 16, 128)
    upper = jnp.dot(everything, first, preferred_element_type=F32)
    lower = jnp.dot(everything, second, preferred_element_type=F32)
    column = slot[0:XL]
    for dd in range(NGX):
        block = jnp.concatenate([upper[16 * dd:16 * dd + 16], lower[16 * dd:16 * dd + 8]], axis=0)
        stack = [jnp.where(column == zz, block, 0.0) for zz in range(ZZ)] + [jnp.zeros((8, 256), F32)]
        bd[128 * dd:128 * dd + 128, :] = jnp.concatenate(stack, axis=0).astype(BF16)

    for k in range(NGX // 2):
        sides = []
        for dd in (2 * k, 2 * k + 1):
            if dd:
                acopies[dd].wait_recv()
            held = (arecv if dd else asend)[dd].astype(F32)
            sides.append(decode(held) * held[SHARE:SHARE + 1, :])
        high, rest = split(jnp.concatenate(sides, axis=1))
        product = jnp.dot(jnp.concatenate([high, rest], axis=0), bd[256 * k:256 * k + 256, :], preferred_element_type=F32)
        if k == 0:
            acc[...] = product
        else:
            acc[...] += product

    core = acc[0:80, :] + acc[80:160, :]
    for zz in range(ZZ):
        d2[80 * zz:80 * zz + 80, 0:RI] = core[:, RI * zz:RI * zz + RI]
    rows = jnp.concatenate([d2[pl.ds(c, ZL, stride=8), :][:, 0:RI] for c in range(SHARE)], axis=1)
    unit = scale_of(jnp.max(jnp.abs(rows), keepdims=True))
    words = jnp.concatenate([encode(rows, 1.0 / unit), jnp.broadcast_to(unit, (ZL, 96))], axis=1)
    cbuf[gz] = words.astype(BF16)

    ccopies = [
        pltpu.make_async_remote_copy(cbuf.at[gz], cbuf.at[gz], cs_sem.at[e], cr_sem.at[e], device_id=to_gz(e), device_id_type=MESH)
        for e in range(1, NGZ)
    ]
    for copy in ccopies:
        copy.start()
    for copy in ccopies:
        copy.wait_recv()

    real = lax.broadcasted_iota(jnp.int32, (ZL, 384), 1) < SHARE * RI
    for z0 in range(NGZ):
        held = cbuf[z0].astype(F32)
        high, rest = split(jnp.where(real, decode(held) * held[:, 288:289], 0.0))
        chi[ZL * z0:ZL * z0 + ZL, :] = high
        clo[ZL * z0:ZL * z0 + ZL, :] = rest
    own = pl.ds(pl.multiple_of(gz * ZL, 16), ZL)
    left = jnp.concatenate([chi[own, :], clo[own, :]], axis=0)
    gram = lax.dot_general(left, chi[...], NT, preferred_element_type=F32) + lax.dot_general(left, clo[...], NT, preferred_element_type=F32)
    gram = (gram[0:ZL] + gram[ZL:2 * ZL]) * (1.0 / (RI * RJ * RP))
    for a in range(6):
        for b in range(3):
            gpart[3 * a + b] = gram[8 * a:8 * a + 8, 128 * b:128 * b + 128]

    reducer = (gy == 0) | (gx % 8 == 0)
    tile = jnp.where(gy == 0, gx, 16 + gx // 8)

    def shipment(r):
        there = {"gx": r, "gz": gz, "gy": 0} if r < 16 else {"gx": 8 * (r - 16), "gz": gz, "gy": 1}
        return pltpu.make_async_remote_copy(gpart.at[r], rrecv.at[line], rs_sem.at[r], rr_sem, device_id=there, device_id_type=MESH)

    for r in range(18):
        @pl.when(jnp.logical_not(reducer & (tile == r)))
        def _():
            shipment(r).start()

    def spread_out(k):
        return pltpu.make_async_remote_copy(red, ofull.at[tile], bs_sem.at[k], br_sem.at[tile], device_id=to_line(k), device_id_type=MESH)

    @pl.when(reducer)
    def _():
        rrecv[line] = gpart[tile]
        rest = rrecv.at[pl.ds(0, 31)]
        pltpu.make_async_copy(rest, rest, rr_sem).wait()
        summed = rrecv[0]
        for k in range(1, 32):
            summed = summed + rrecv[k]
        red[...] = summed
        ofull[tile] = summed

        def send(k, _):
            spread_out(k).start()
            return 0

        lax.fori_loop(1, 32, send, 0)

    for r in range(18):
        @pl.when(jnp.logical_not(reducer & (tile == r)))
        def _():
            pltpu.make_async_copy(ofull.at[r], ofull.at[r], br_sem.at[r]).wait()

    for a in range(6):
        for b in range(3):
            out[8 * a:8 * a + 8, 128 * b:128 * b + 128] = ofull[3 * a + b]

    for copy in xcopies + exchanges + list(acopies.values()) + ccopies:
        copy.wait_send()
    for r in range(18):
        @pl.when(jnp.logical_not(reducer & (tile == r)))
        def _():
            shipment(r).wait_send()

    @pl.when(reducer)
    def _():
        def finish(k, _):
            spread_out(k).wait_send()
            return 0

        lax.fori_loop(1, 32, finish, 0)


def body(field, x_factor, y_factor, species_basis_matrix):
    vmem = pl.BlockSpec(memory_space=pltpu.VMEM)
    dma = pltpu.SemaphoreType.DMA
    return pl.pallas_call(
        kernel,
        out_shape=jax.ShapeDtypeStruct((ZL, NGZ * ZL), F32),
        in_specs=[pl.BlockSpec(memory_space=pl.ANY), vmem, vmem, vmem],
        out_specs=vmem,
        scratch_shapes=[
            pltpu.VMEM((NS, XL, ZL, 128), BF16),
            pltpu.VMEM((1024, 256), BF16),
            pltpu.VMEM((1024, 256), BF16),
            pltpu.VMEM((XL * ZL, 128), F32),
            pltpu.VMEM((XL * ZL, 128), F32),
            pltpu.VMEM((XL * ZL, 128), F32),
            pltpu.VMEM((XL * ZL, 128), F32),
            pltpu.VMEM((16, 128), BF16),
            pltpu.VMEM((NGX, 16, 128), BF16),
            pltpu.VMEM((NGX * 128, 256), BF16),
            pltpu.VMEM((NGX, 80, 128), BF16),
            pltpu.VMEM((NGX, 80, 128), BF16),
            pltpu.VMEM((160, 256), F32),
            pltpu.VMEM((400, 128), F32),
            pltpu.VMEM((NGZ, ZL, 384), BF16),
            pltpu.VMEM((NGZ * ZL, 384), BF16),
            pltpu.VMEM((NGZ * ZL, 384), BF16),
            pltpu.VMEM((18, 8, 128), F32),
            pltpu.VMEM((32, 8, 128), F32),
            pltpu.VMEM((8, 128), F32),
            pltpu.VMEM((18, 8, 128), F32),
            dma((CH,)), dma((CH,)), dma((CH,)), dma((NGX,)), dma((NGX,)), dma((NGX,)), dma((NGX,)),
            dma((NGZ,)), dma((NGZ,)), dma((18,)), dma, dma((32,)), dma((18,)),
        ],
        compiler_params=pltpu.CompilerParams(collective_id=0, has_side_effects=True, vmem_limit_bytes=40 * 1024 * 1024),
    )(field, x_factor, y_factor, species_basis_matrix)


def solution(mesh):
    placed = (P(None, "gx", "gz", "gy"), P("gx", None), P("gy", None), P())
    return jax.shard_map(body, mesh=mesh, in_specs=placed, out_specs=P("gz", None), check_vma=False)
```

```python
import functools

import jax
import jax.numpy as jnp
from jax import lax
from jax.experimental import pallas as pl
from jax.experimental.pallas import tpu as pltpu
from jax.sharding import PartitionSpec as P

MESH = pl.DeviceIdType.MESH
F32 = jnp.float32
BF16 = jnp.bfloat16
NT = (((1,), (1,)), ((), ()))

NGX, NGZ, NGY = 16, 8, 2
XL, ZL = 24, 48
RI, RJ, RP, NS = 48, 48, 4, 8
ZG, ZZ = 10, 5
TOP = 32000.0
BIAS = 124.0
SHARE = 6
CH = 4
ROWS = XL * ZL // CH
FAR = (4, 12, 3, 11, 5, 13, 2, 10, 6, 14, 1, 9, 7, 15, 8)


def encode(value, inverse):
    whole = jnp.round(value * inverse)
    size = jnp.abs(whole)
    high = jnp.floor(size * (1.0 / 128.0))
    code = jnp.exp2(high - BIAS) * (1.0 + (size - 128.0 * high) * (1.0 / 128.0))
    return jnp.where(whole < 0.0, -code, code)


def decode(code):
    size = jnp.abs(code)
    high = jnp.floor(jnp.log2(size) + 0.002)
    whole = jnp.round(128.0 * (high + (BIAS - 1.0) + size * jnp.exp2(-high)))
    return jnp.where(code < 0.0, -whole, whole)


def scale_of(largest):
    unit = (largest * (1.01 / TOP)).astype(BF16).astype(F32)
    return jnp.maximum(unit, 2.0**-100)


def split(value):
    high = value.astype(BF16)
    return high, (value - high.astype(F32)).astype(BF16)


def kernel(field, xf_hbm, yf_hbm, sb_hbm, out, fbuf, xf, yf, sb, whi, wlo, mine, other, prt, tsum, xsend, xrecv, bd, asend, arecv,
           acc, d2, csend, owns, theirs, left_buf, right_buf, gsum, fin,
           f_sem, p_sem, es_sem, er_sem, xs_sem, xr_sem, as_sem, ar_sem, cs_sem, cr_sem, gs_sem, gr_sem, qs_sem, qr_sem):
    gx, gz, gy = lax.axis_index("gx"), lax.axis_index("gz"), lax.axis_index("gy")
    y_lo, z_at = gx // 8, gx % 8
    quad = y_lo * 2 + gy
    x_at, y_hi = gz // 2, gz % 2

    def to_gx(dd):
        return {"gx": (gx + dd) % NGX, "gz": gz, "gy": gy}

    def in_quad(dy, dc):
        return {"gx": (y_lo + dy) % 2 * 8 + z_at, "gz": gz, "gy": (gy + dc) % 2}

    def quad_of(dy, dc):
        return (y_lo + dy) % 2 * 2 + (gy + dc) % 2

    def charged(dx, dh):
        return {"gx": x_at // 2 * 8 + z_at, "gz": (x_at + dx) % 4 * 2 + (y_hi + dh) % 2, "gy": x_at % 2}

    params = [pltpu.make_async_copy(a, b, p_sem.at[k]) for k, (a, b) in enumerate(((xf_hbm, xf), (yf_hbm, yf), (sb_hbm, sb)))]
    for copy in params:
        copy.start()
    loads = []
    for c in range(CH):
        part = pl.ds(c * (XL // CH), XL // CH)
        loads.append(pltpu.make_async_copy(field.at[:, part], fbuf.at[:, part], f_sem.at[c]))
        loads[-1].start()

    barrier = pltpu.get_barrier_semaphore()

    for dd in range(1, NGX):
        pl.semaphore_signal(barrier, inc=1, device_id=to_gx(dd), device_id_type=MESH)
    for dy in range(2):
        pl.semaphore_signal(barrier, inc=1, device_id=in_quad(dy, 1), device_id_type=MESH)
    for b in range(2):
        @pl.when(2 * quad + b != gz)
        def _():
            for w in range(4):
                there = {"gx": w // 2 * 8 + z_at, "gz": 2 * quad + b, "gy": w % 2}
                pl.semaphore_signal(barrier, inc=1, device_id=there, device_id_type=MESH)

    for copy in params:
        copy.wait()

    x32 = xf[...].astype(F32)
    low = jnp.concatenate([x32[16:24], jnp.zeros((8, RI), F32)], axis=0)
    gap = jnp.zeros((16, 16), F32)
    xsend[...] = jnp.concatenate([x32[0:16], gap, low, gap], axis=1).astype(BF16)

    lane = lax.broadcasted_iota(jnp.int32, (RJ, 256), 1)
    q = lane & 7
    dest = (gx + ((lane >> 3) & 15)) & 15
    late = (q >= 3).astype(jnp.int32)
    jl = 3 * dest + q - 3 * late
    pick = (lax.broadcasted_iota(jnp.int32, (RJ, 256), 0) == jl) & (q < SHARE)
    spread = lax.dot_general(yf[...], pick.astype(F32).astype(BF16), (((0,), (0,)), ((), ())), preferred_element_type=F32)
    plane = (2 * (((lane >> 7) + gy) & 1) + late)[0:1]
    basis = sb[...]
    for s in range(NS):
        mix = jnp.zeros((1, 256), F32)
        for p in range(RP):
            mix = mix + jnp.where(plane == p, basis[p:p + 1, s:s + 1], 0.0)
        high, rest = split(spread * mix)
        whi[128 * s:128 * s + 128, :] = high
        wlo[128 * s:128 * s + 128, :] = rest

    exchanges = []
    for c in range(CH):
        loads[c].wait()
        left = jnp.concatenate(
            [fbuf[s, c * (XL // CH):(c + 1) * (XL // CH)].reshape(ROWS, 128) for s in range(NS)], axis=1)
        part = jnp.dot(left, whi[...], preferred_element_type=F32) + jnp.dot(left, wlo[...], preferred_element_type=F32)
        span = pl.ds(c * ROWS, ROWS)
        mine[span, :] = part[:, 0:128]
        other[span, :] = part[:, 128:256]
        exchanges.append(pltpu.make_async_remote_copy(
            other.at[span], prt.at[span], es_sem.at[c], er_sem.at[c], device_id=in_quad(0, 1), device_id_type=MESH))

    pl.semaphore_wait(barrier, NGX - 1 + 2 + NGZ - 1)
    for copy in exchanges:
        copy.start()
    xcopies = [
        pltpu.make_async_remote_copy(xsend, xrecv.at[dd], xs_sem.at[dd], xr_sem.at[dd], device_id=to_gx(dd), device_id_type=MESH)
        for dd in FAR
    ]
    for copy in xcopies:
        copy.start()

    largest = jnp.zeros((8, 128), F32)
    for c in range(CH):
        exchanges[c].wait_recv()
        span = pl.ds(c * ROWS, ROWS)
        total = mine[span, :] + prt[span, :]
        tsum[span, :] = total
        largest = jnp.maximum(largest, jnp.max(jnp.abs(total).reshape(ROWS // 8, 8, 128), axis=0))
    unit = scale_of(jnp.max(largest, keepdims=True))
    inverse = 1.0 / unit

    is_scale = lax.broadcasted_iota(jnp.int32, (NGX, 8, 128), 1) == SHARE

    def coded(zg):
        pieces = []
        for zz in range(ZZ):
            z = zg + ZG * zz
            pieces.append(tsum[pl.ds(z, XL, stride=ZL), :] if z < ZL else jnp.zeros((XL, 128), F32))
        pieces.append(jnp.zeros((8, 128), F32))
        tile = jnp.concatenate(pieces, axis=0).T
        return jnp.where(is_scale, unit.reshape(1, 1, 1), encode(tile, inverse).reshape(NGX, 8, 128))

    for m in range(ZG // 2):
        both = jnp.concatenate([coded(2 * m), coded(2 * m + 1)], axis=1)
        asend[:, 16 * m:16 * m + 16, :] = both.astype(BF16)

    acopies = {
        dd: pltpu.make_async_remote_copy(asend.at[dd], arecv.at[dd], as_sem.at[dd], ar_sem.at[dd], device_id=to_gx(dd), device_id_type=MESH)
        for dd in range(1, NGX)
    }
    for dd in FAR:
        acopies[dd].start()

    for copy in xcopies:
        copy.wait_recv()
    xrecv[0] = xsend[...]
    row = lax.broadcasted_iota(jnp.int32, (128, 256), 0)
    lane = lax.broadcasted_iota(jnp.int32, (128, 256), 1)
    slot = jnp.zeros((128, 256), jnp.int32)
    for zz in range(1, ZZ):
        slot = slot + (lane >= RI * zz).astype(jnp.int32)
    want = lane - RI * slot
    first = ((row == want) & (lane < RI * ZZ)).astype(F32).astype(BF16)
    second = ((row == want + 64) & (lane < RI * ZZ)).astype(F32).astype(BF16)
    everything = xrecv[...].reshape(NGX * 16, 128)
    upper = jnp.dot(everything, first, preferred_element_type=F32)
    lower = jnp.dot(everything, second, preferred_element_type=F32)
    column = slot[0:XL]
    for dd in range(NGX):
        block = jnp.concatenate([upper[16 * dd:16 * dd + 16], lower[16 * dd:16 * dd + 8]], axis=0)
        stack = [jnp.where(column == zz, block, 0.0) for zz in range(ZZ)] + [jnp.zeros((8, 256), F32)]
        bd[128 * dd:128 * dd + 128, :] = jnp.concatenate(stack, axis=0).astype(BF16)

    for k in range(NGX // 2):
        sides = []
        for dd in (2 * k, 2 * k + 1):
            if dd:
                acopies[dd].wait_recv()
            held = (arecv if dd else asend)[dd].astype(F32)
            sides.append(decode(held) * held[SHARE:SHARE + 1, :])
        high, rest = split(jnp.concatenate(sides, axis=1))
        product = jnp.dot(jnp.concatenate([high, rest], axis=0), bd[256 * k:256 * k + 256, :], preferred_element_type=F32)
        if k == 0:
            acc[...] = product
        else:
            acc[...] += product

    core = acc[0:80, :] + acc[80:160, :]
    for zz in range(ZZ):
        d2[80 * zz:80 * zz + 80, 0:RI] = core[:, RI * zz:RI * zz + RI]
    rows = jnp.concatenate([d2[pl.ds(c, ZL, stride=8), :][:, 0:RI] for c in range(SHARE)], axis=1)
    unit = scale_of(jnp.max(jnp.abs(rows), keepdims=True))
    words = jnp.concatenate([encode(rows, 1.0 / unit), jnp.broadcast_to(unit, (ZL, 96))], axis=1)
    csend[...] = words.astype(BF16)

    ccopies = []
    for dx, dh in ((2, 1), (1, 1), (3, 1), (0, 1), (2, 0), (1, 0), (3, 0)):
        k = 2 * dx + dh
        ccopies.append(pltpu.make_async_remote_copy(
            csend, theirs.at[4 * y_hi + quad], cs_sem.at[k], cr_sem.at[4 + 4 * y_hi + quad], device_id=charged(dx, dh), device_id_type=MESH))
    for dy, dc in ((1, 1), (1, 0), (0, 1)):
        ccopies.append(pltpu.make_async_remote_copy(
            csend, owns.at[quad], cs_sem.at[8 + 2 * dy + dc], cr_sem.at[quad], device_id=in_quad(dy, dc), device_id_type=MESH))
    for copy in ccopies:
        copy.start()
    owns[quad] = csend[...]
    real = lax.broadcasted_iota(jnp.int32, (ZL, 384), 1) < SHARE * RI

    def opened(words):
        held = words.astype(F32)
        return split(jnp.where(real, decode(held) * held[:, 288:289], 0.0))

    for dy, dc in ((0, 1), (1, 0), (1, 1)):
        w = quad_of(dy, dc)
        pltpu.make_async_copy(owns.at[w], owns.at[w], cr_sem.at[w]).wait()
    for w in range(4):
        left_buf[0:ZL, 384 * w:384 * w + 384], left_buf[ZL:2 * ZL, 384 * w:384 * w + 384] = opened(owns[w])
    for b in range(2):
        @pl.when(2 * quad + b != gz)
        def _():
            for w in range(4):
                k = 4 * b + w
                pltpu.make_async_copy(theirs.at[k], theirs.at[k], cr_sem.at[4 + k]).wait()

        @pl.when(2 * quad + b == gz)
        def _():
            for w in range(4):
                theirs[4 * b + w] = owns[w]

        for w in range(4):
            at = pl.ds(384 * w, 384)
            right_buf[ZL * b:ZL * b + ZL, at], right_buf[128 + ZL * b:128 + ZL * b + ZL, at] = opened(theirs[4 * b + w])
    right_buf[96:128, :] = jnp.zeros((32, 1536), BF16)
    right_buf[224:256, :] = jnp.zeros((32, 1536), BF16)
    gram = lax.dot_general(left_buf[...], right_buf[...], NT, preferred_element_type=F32)
    gram = (gram[0:ZL] + gram[ZL:2 * ZL]) * (1.0 / (RI * RJ * RP))
    gsum[z_at] = gram[:, 0:128] + gram[:, 128:256]

    gcopies = [
        pltpu.make_async_remote_copy(
            gsum.at[z_at], gsum.at[z_at], gs_sem.at[dz], gr_sem.at[z_at],
            device_id={"gx": y_lo * 8 + (z_at + dz) % 8, "gz": gz, "gy": gy}, device_id_type=MESH)
        for dz in (4, 3, 5, 2, 6, 1, 7)
    ]
    for copy in gcopies:
        copy.start()
    for dz in (7, 1, 6, 2, 5, 3, 4):
        w = (z_at + dz) % 8
        pltpu.make_async_copy(gsum.at[w], gsum.at[w], gr_sem.at[w]).wait()
    total = gsum[0]
    for k in range(1, 8):
        total = total + gsum[k]
    fin[quad] = total

    qcopies = [
        pltpu.make_async_remote_copy(
            fin.at[quad], fin.at[quad], qs_sem.at[2 * dy + dc], qr_sem.at[quad], device_id=in_quad(dy, dc), device_id_type=MESH)
        for dy, dc in ((1, 1), (1, 0), (0, 1))
    ]
    for copy in qcopies:
        copy.start()
    for dy, dc in ((0, 1), (1, 0), (1, 1)):
        w = quad_of(dy, dc)
        pltpu.make_async_copy(fin.at[w], fin.at[w], qr_sem.at[w]).wait()
    out[...] = jnp.concatenate([fin[w][:, 0:96] for w in range(4)], axis=1)

    for copy in xcopies + exchanges + list(acopies.values()) + ccopies + gcopies + qcopies:
        copy.wait_send()


def body(field, x_factor, y_factor, species_basis_matrix):
    vmem = pl.BlockSpec(memory_space=pltpu.VMEM)
    dma = pltpu.SemaphoreType.DMA
    return pl.pallas_call(
        kernel,
        out_shape=jax.ShapeDtypeStruct((ZL, NGZ * ZL), F32),
        in_specs=[pl.BlockSpec(memory_space=pltpu.HBM)] * 4,
        out_specs=vmem,
        scratch_shapes=[
            pltpu.VMEM((NS, XL, ZL, 128), BF16),
            pltpu.VMEM((XL, RI), BF16),
            pltpu.VMEM((RJ, 128), BF16),
            pltpu.VMEM((RP, NS), F32),
            pltpu.VMEM((1024, 256), BF16),
            pltpu.VMEM((1024, 256), BF16),
            pltpu.VMEM((XL * ZL, 128), F32),
            pltpu.VMEM((XL * ZL, 128), F32),
            pltpu.VMEM((XL * ZL, 128), F32),
            pltpu.VMEM((XL * ZL, 128), F32),
            pltpu.VMEM((16, 128), BF16),
            pltpu.VMEM((NGX, 16, 128), BF16),
            pltpu.VMEM((NGX * 128, 256), BF16),
            pltpu.VMEM((NGX, 80, 128), BF16),
            pltpu.VMEM((NGX, 80, 128), BF16),
            pltpu.VMEM((160, 256), F32),
            pltpu.VMEM((400, 128), F32),
            pltpu.VMEM((ZL, 384), BF16),
            pltpu.VMEM((4, ZL, 384), BF16),
            pltpu.VMEM((8, ZL, 384), BF16),
            pltpu.VMEM((96, 1536), BF16),
            pltpu.VMEM((256, 1536), BF16),
            pltpu.VMEM((8, ZL, 128), F32),
            pltpu.VMEM((4, ZL, 128), F32),
            dma((CH,)), dma((3,)), dma((CH,)), dma((CH,)), dma((NGX,)), dma((NGX,)), dma((NGX,)), dma((NGX,)),
            dma((12,)), dma((12,)), dma((8,)), dma((8,)), dma((4,)), dma((4,)),
        ],
        compiler_params=pltpu.CompilerParams(collective_id=0, has_side_effects=True, vmem_limit_bytes=56 * 1024 * 1024),
    )(field, x_factor, y_factor.T, species_basis_matrix.T)


def solution(mesh):
    placed = (P(None, "gx", "gz", "gy"), P("gx", None), P("gy", None), P())
    return jax.shard_map(body, mesh=mesh, in_specs=placed, out_specs=P("gz", None), check_vma=False)
```

```python
import functools

import jax
import jax.numpy as jnp
from jax import lax
from jax.experimental import pallas as pl
from jax.experimental.pallas import tpu as pltpu
from jax.sharding import PartitionSpec as P

MESH = pl.DeviceIdType.MESH
F32 = jnp.float32
BF16 = jnp.bfloat16
NT = (((1,), (1,)), ((), ()))

NGX, NGZ, NGY = 16, 8, 2
XL, ZL = 24, 48
RI, RJ, RP, NS = 48, 48, 4, 8
ZG, ZZ = 10, 5
TOP = 32000.0
BIAS = 124.0
SHARE = 6
CH = 4
ROWS = XL * ZL // CH
FAR = (4, 12, 3, 11, 5, 13, 2, 10, 6, 14, 1, 9, 7, 15, 8)


def encode(value, inverse):
    whole = jnp.round(value * inverse)
    size = jnp.abs(whole)
    high = jnp.floor(size * (1.0 / 128.0))
    code = jnp.exp2(high - BIAS) * (1.0 + (size - 128.0 * high) * (1.0 / 128.0))
    return jnp.where(whole < 0.0, -code, code)


def decode(code):
    size = jnp.abs(code)
    high = jnp.floor(jnp.log2(size) + 0.002)
    whole = jnp.round(128.0 * (high + (BIAS - 1.0) + size * jnp.exp2(-high)))
    return jnp.where(code < 0.0, -whole, whole)


def scale_of(largest):
    unit = (largest * (1.01 / TOP)).astype(BF16).astype(F32)
    return jnp.maximum(unit, 2.0**-100)


def split(value):
    high = value.astype(BF16)
    return high, (value - high.astype(F32)).astype(BF16)


def kernel(field, xf_hbm, yf_hbm, sb_hbm, out, fbuf, xf, yf, sb, whi, wlo, mine, other, prt, tsum, xsend, xrecv, bd, asend, arecv,
           acc, d2, csend, owns, theirs, left_buf, right_buf, gsum, fin,
           f_sem, p_sem, es_sem, er_sem, xs_sem, xr_sem, as_sem, ar_sem, cs_sem, cr_sem, gs_sem, gr_sem, qs_sem, qr_sem):
    gx, gz, gy = lax.axis_index("gx"), lax.axis_index("gz"), lax.axis_index("gy")
    y_lo, z_at = gx // 8, gx % 8
    quad = y_lo * 2 + gy
    x_at, y_hi = gz // 2, gz % 2

    def to_gx(dd):
        return {"gx": (gx + dd) % NGX, "gz": gz, "gy": gy}

    def in_quad(dy, dc):
        return {"gx": (y_lo + dy) % 2 * 8 + z_at, "gz": gz, "gy": (gy + dc) % 2}

    def quad_of(dy, dc):
        return (y_lo + dy) % 2 * 2 + (gy + dc) % 2

    def charged(dx, dh):
        return {"gx": x_at // 2 * 8 + z_at, "gz": (x_at + dx) % 4 * 2 + (y_hi + dh) % 2, "gy": x_at % 2}

    barrier = pltpu.get_barrier_semaphore()

    for dd in FAR:
        pl.semaphore_signal(barrier, inc=1, device_id=to_gx(dd), device_id_type=MESH)
    for dy in range(2):
        pl.semaphore_signal(barrier, inc=1, device_id=in_quad(dy, 1), device_id_type=MESH)
    for b in range(2):
        @pl.when(2 * quad + b != gz)
        def _():
            for w in range(4):
                there = {"gx": w // 2 * 8 + z_at, "gz": 2 * quad + b, "gy": w % 2}
                pl.semaphore_signal(barrier, inc=1, device_id=there, device_id_type=MESH)

    params = [pltpu.make_async_copy(a, b, p_sem.at[k]) for k, (a, b) in enumerate(((xf_hbm, xf), (yf_hbm, yf), (sb_hbm, sb)))]
    for copy in params:
        copy.start()
    loads = []
    for c in range(CH):
        part = pl.ds(c * (XL // CH), XL // CH)
        loads.append(pltpu.make_async_copy(field.at[:, part], fbuf.at[:, part], f_sem.at[c]))
        loads[-1].start()

    for copy in params:
        copy.wait()

    x32 = xf[...].astype(F32)
    low = jnp.concatenate([x32[16:24], jnp.zeros((8, RI), F32)], axis=0)
    gap = jnp.zeros((16, 16), F32)
    xsend[...] = jnp.concatenate([x32[0:16], gap, low, gap], axis=1).astype(BF16)

    lane = lax.broadcasted_iota(jnp.int32, (RJ, 256), 1)
    q = lane & 7
    dest = (gx + ((lane >> 3) & 15)) & 15
    late = (q >= 3).astype(jnp.int32)
    jl = 3 * dest + q - 3 * late
    pick = (lax.broadcasted_iota(jnp.int32, (RJ, 256), 0) == jl) & (q < SHARE)
    spread = lax.dot_general(yf[...], pick.astype(F32).astype(BF16), (((0,), (0,)), ((), ())), preferred_element_type=F32)
    plane = (2 * (((lane >> 7) + gy) & 1) + late)[0:1]
    basis = sb[...]
    for s in range(NS):
        mix = jnp.zeros((1, 256), F32)
        for p in range(RP):
            mix = mix + jnp.where(plane == p, basis[p:p + 1, s:s + 1], 0.0)
        high, rest = split(spread * mix)
        whi[128 * s:128 * s + 128, :] = high
        wlo[128 * s:128 * s + 128, :] = rest

    spare = lax.broadcasted_iota(jnp.int32, (ROWS, 128), 1) & 7
    exchanges = []
    for c in range(CH):
        loads[c].wait()
        left = jnp.concatenate(
            [fbuf[s, c * (XL // CH):(c + 1) * (XL // CH)].reshape(ROWS, 128) for s in range(NS)], axis=1)
        part = jnp.dot(left, whi[...], preferred_element_type=F32) + jnp.dot(left, wlo[...], preferred_element_type=F32)
        span = pl.ds(c * ROWS, ROWS)
        mine[span, :] = part[:, 0:128]
        unit = scale_of(jnp.max(jnp.abs(part[:, 128:256]), keepdims=True))
        other[span, :] = jnp.where(spare == SHARE, unit, encode(part[:, 128:256], 1.0 / unit)).astype(BF16)
        exchanges.append(pltpu.make_async_remote_copy(
            other.at[span], prt.at[span], es_sem.at[c], er_sem.at[c], device_id=in_quad(0, 1), device_id_type=MESH))

    pl.semaphore_wait(barrier, NGX - 1 + 2 + NGZ - 1)
    for copy in exchanges:
        copy.start()
    xcopies = [
        pltpu.make_async_remote_copy(xsend, xrecv.at[dd], xs_sem.at[dd], xr_sem.at[dd], device_id=to_gx(dd), device_id_type=MESH)
        for dd in FAR
    ]
    for copy in xcopies:
        copy.start()

    largest = jnp.zeros((8, 128), F32)
    for c in range(CH):
        exchanges[c].wait_recv()
        span = pl.ds(c * ROWS, ROWS)
        came = prt[span, :].astype(F32)
        total = mine[span, :] + jnp.where(spare < SHARE, decode(came) * came[0:1, SHARE:SHARE + 1], 0.0)
        tsum[span, :] = total
        largest = jnp.maximum(largest, jnp.max(jnp.abs(total).reshape(ROWS // 8, 8, 128), axis=0))
    unit = scale_of(jnp.max(largest, keepdims=True))
    inverse = 1.0 / unit

    line = lax.broadcasted_iota(jnp.int32, (NGX, 8, 128), 1)

    def coded(zg):
        pieces = []
        for zz in range(ZZ):
            z = zg + ZG * zz
            pieces.append(tsum[pl.ds(z, XL, stride=ZL), :] if z < ZL else jnp.zeros((XL, 128), F32))
        pieces.append(jnp.zeros((8, 128), F32))
        return encode(jnp.concatenate(pieces, axis=0).T, inverse).reshape(NGX, 8, 128)

    tails = (coded(8), coded(9))

    def packed(zg):
        if zg < 6:
            return jnp.where(line < SHARE, coded(zg), pltpu.roll(tails[zg // 3], 6 - 2 * (zg % 3), axis=1))
        return jnp.where(line == SHARE, unit.reshape(1, 1, 1), coded(zg))

    for m in range(4):
        asend[:, 16 * m:16 * m + 16, :] = jnp.concatenate([packed(2 * m), packed(2 * m + 1)], axis=1).astype(BF16)

    acopies = {
        dd: pltpu.make_async_remote_copy(asend.at[dd], arecv.at[dd], as_sem.at[dd], ar_sem.at[dd], device_id=to_gx(dd), device_id_type=MESH)
        for dd in range(1, NGX)
    }
    for dd in FAR:
        acopies[dd].start()

    for copy in xcopies:
        copy.wait_recv()
    xrecv[0] = xsend[...]
    row = lax.broadcasted_iota(jnp.int32, (128, 256), 0)
    lane = lax.broadcasted_iota(jnp.int32, (128, 256), 1)
    slot = jnp.zeros((128, 256), jnp.int32)
    for zz in range(1, ZZ):
        slot = slot + (lane >= RI * zz).astype(jnp.int32)
    want = lane - RI * slot
    first = ((row == want) & (lane < RI * ZZ)).astype(F32).astype(BF16)
    second = ((row == want + 64) & (lane < RI * ZZ)).astype(F32).astype(BF16)
    everything = xrecv[...].reshape(NGX * 16, 128)
    upper = jnp.dot(everything, first, preferred_element_type=F32)
    lower = jnp.dot(everything, second, preferred_element_type=F32)
    column = slot[0:XL]
    for dd in range(NGX):
        block = jnp.concatenate([upper[16 * dd:16 * dd + 16], lower[16 * dd:16 * dd + 8]], axis=0)
        stack = [jnp.where(column == zz, block, 0.0) for zz in range(ZZ)] + [jnp.zeros((8, 256), F32)]
        bd[128 * dd:128 * dd + 128, :] = jnp.concatenate(stack, axis=0).astype(BF16)

    eight = lax.broadcasted_iota(jnp.int32, (8, 128), 0)
    for k in range(NGX // 2):
        sides = []
        for dd in (2 * k, 2 * k + 1):
            if dd:
                acopies[dd].wait_recv()
            held = (arecv if dd else asend)[dd].astype(F32)
            value = decode(held) * held[48 + SHARE:48 + SHARE + 1, :]
            tails = []
            for t in range(2):
                a, b, c = (pltpu.roll(value[24 * t + 8 * n:24 * t + 8 * n + 8], 2 * n + 2, axis=0) for n in range(3))
                tails.append(jnp.where(eight < 2, a, jnp.where(eight < 4, b, c)))
            sides.append(jnp.concatenate([value] + tails, axis=0))
        high, rest = split(jnp.concatenate(sides, axis=1))
        product = jnp.dot(jnp.concatenate([high, rest], axis=0), bd[256 * k:256 * k + 256, :], preferred_element_type=F32)
        if k == 0:
            acc[...] = product
        else:
            acc[...] += product

    core = acc[0:80, :] + acc[80:160, :]
    for zz in range(ZZ):
        d2[80 * zz:80 * zz + 80, 0:RI] = core[:, RI * zz:RI * zz + RI]
    rows = jnp.concatenate([d2[pl.ds(c, ZL, stride=8), :][:, 0:RI] for c in range(SHARE)], axis=1)
    unit = scale_of(jnp.max(jnp.abs(rows), keepdims=True))
    words = encode(rows, 1.0 / unit)
    rest = [words[16 * k:16 * k + 16, 256:288] for k in range(3)] + [jnp.broadcast_to(unit, (16, 32))]
    csend[...] = jnp.concatenate([words[:, 0:128], words[:, 128:256], jnp.concatenate(rest, axis=1)], axis=0).astype(BF16)

    ccopies = []
    for dx, dh in ((2, 1), (1, 1), (3, 1), (0, 1), (2, 0), (1, 0), (3, 0)):
        k = 2 * dx + dh
        ccopies.append(pltpu.make_async_remote_copy(
            csend, theirs.at[4 * y_hi + quad], cs_sem.at[k], cr_sem.at[4 + 4 * y_hi + quad], device_id=charged(dx, dh), device_id_type=MESH))
    for dy, dc in ((1, 1), (1, 0), (0, 1)):
        ccopies.append(pltpu.make_async_remote_copy(
            csend, owns.at[quad], cs_sem.at[8 + 2 * dy + dc], cr_sem.at[quad], device_id=in_quad(dy, dc), device_id_type=MESH))
    for copy in ccopies:
        copy.start()
    owns[quad] = csend[...]

    def opened(pieces, buf, at, low):
        rests = []
        for w in range(4):
            held = pieces[w].astype(F32)
            value = decode(held) * held[96:97, 96:97]
            for k in range(2):
                lanes = pl.ds(256 * w + 128 * k, 128)
                buf[at:at + ZL, lanes], buf[low:low + ZL, lanes] = split(value[ZL * k:ZL * k + ZL])
            rests.append(jnp.concatenate([value[96:112, 32 * k:32 * k + 32] for k in range(3)], axis=0))
        buf[at:at + ZL, 1024:1152], buf[low:low + ZL, 1024:1152] = split(jnp.concatenate(rests, axis=1))

    for dy, dc in ((0, 1), (1, 0), (1, 1)):
        w = quad_of(dy, dc)
        pltpu.make_async_copy(owns.at[w], owns.at[w], cr_sem.at[w]).wait()
    opened([owns[w] for w in range(4)], left_buf, 0, ZL)
    for b in range(2):
        @pl.when(2 * quad + b != gz)
        def _():
            for w in range(4):
                k = 4 * b + w
                pltpu.make_async_copy(theirs.at[k], theirs.at[k], cr_sem.at[4 + k]).wait()

        @pl.when(2 * quad + b == gz)
        def _():
            for w in range(4):
                theirs[4 * b + w] = owns[w]

        opened([theirs[4 * b + w] for w in range(4)], right_buf, ZL * b, 128 + ZL * b)
    right_buf[96:128, :] = jnp.zeros((32, 1152), BF16)
    right_buf[224:256, :] = jnp.zeros((32, 1152), BF16)
    gram = lax.dot_general(left_buf[...], right_buf[...], NT, preferred_element_type=F32)
    gram = (gram[0:ZL] + gram[ZL:2 * ZL]) * (1.0 / (RI * RJ * RP))
    gram = gram[:, 0:128] + gram[:, 128:256]
    unit = scale_of(jnp.max(jnp.abs(gram), keepdims=True))
    beyond = lax.broadcasted_iota(jnp.int32, (ZL, 128), 1) >= 96
    gsum[z_at] = jnp.where(beyond, unit, encode(gram, 1.0 / unit)).astype(BF16)

    gcopies = [
        pltpu.make_async_remote_copy(
            gsum.at[z_at], gsum.at[z_at], gs_sem.at[dz], gr_sem.at[z_at],
            device_id={"gx": y_lo * 8 + (z_at + dz) % 8, "gz": gz, "gy": gy}, device_id_type=MESH)
        for dz in (4, 3, 5, 2, 6, 1, 7)
    ]
    for copy in gcopies:
        copy.start()
    for dz in (7, 1, 6, 2, 5, 3, 4):
        w = (z_at + dz) % 8
        pltpu.make_async_copy(gsum.at[w], gsum.at[w], gr_sem.at[w]).wait()
    total = jnp.zeros((ZL, 128), F32)
    for k in range(8):
        held = gsum[k].astype(F32)
        total = total + decode(held) * held[:, 96:97]
    fin[quad] = total

    qcopies = [
        pltpu.make_async_remote_copy(
            fin.at[quad], fin.at[quad], qs_sem.at[2 * dy + dc], qr_sem.at[quad], device_id=in_quad(dy, dc), device_id_type=MESH)
        for dy, dc in ((1, 1), (1, 0), (0, 1))
    ]
    for copy in qcopies:
        copy.start()
    for dy, dc in ((0, 1), (1, 0), (1, 1)):
        w = quad_of(dy, dc)
        pltpu.make_async_copy(fin.at[w], fin.at[w], qr_sem.at[w]).wait()
    out[...] = jnp.concatenate([fin[w][:, 0:96] for w in range(4)], axis=1)

    for copy in xcopies + exchanges + list(acopies.values()) + ccopies + gcopies + qcopies:
        copy.wait_send()


def body(field, x_factor, y_factor, species_basis_matrix):
    vmem = pl.BlockSpec(memory_space=pltpu.VMEM)
    dma = pltpu.SemaphoreType.DMA
    return pl.pallas_call(
        kernel,
        out_shape=jax.ShapeDtypeStruct((ZL, NGZ * ZL), F32),
        in_specs=[pl.BlockSpec(memory_space=pltpu.HBM)] * 4,
        out_specs=vmem,
        scratch_shapes=[
            pltpu.VMEM((NS, XL, ZL, 128), BF16),
            pltpu.VMEM((XL, RI), BF16),
            pltpu.VMEM((RJ, 128), BF16),
            pltpu.VMEM((RP, NS), F32),
            pltpu.VMEM((1024, 256), BF16),
            pltpu.VMEM((1024, 256), BF16),
            pltpu.VMEM((XL * ZL, 128), F32),
            pltpu.VMEM((XL * ZL, 128), BF16),
            pltpu.VMEM((XL * ZL, 128), BF16),
            pltpu.VMEM((XL * ZL, 128), F32),
            pltpu.VMEM((16, 128), BF16),
            pltpu.VMEM((NGX, 16, 128), BF16),
            pltpu.VMEM((NGX * 128, 256), BF16),
            pltpu.VMEM((NGX, 64, 128), BF16),
            pltpu.VMEM((NGX, 64, 128), BF16),
            pltpu.VMEM((160, 256), F32),
            pltpu.VMEM((400, 128), F32),
            pltpu.VMEM((112, 128), BF16),
            pltpu.VMEM((4, 112, 128), BF16),
            pltpu.VMEM((8, 112, 128), BF16),
            pltpu.VMEM((96, 1152), BF16),
            pltpu.VMEM((256, 1152), BF16),
            pltpu.VMEM((8, ZL, 128), BF16),
            pltpu.VMEM((4, ZL, 128), F32),
            dma((CH,)), dma((3,)), dma((CH,)), dma((CH,)), dma((NGX,)), dma((NGX,)), dma((NGX,)), dma((NGX,)),
            dma((12,)), dma((12,)), dma((8,)), dma((8,)), dma((4,)), dma((4,)),
        ],
        compiler_params=pltpu.CompilerParams(collective_id=0, has_side_effects=True, vmem_limit_bytes=56 * 1024 * 1024),
    )(field, x_factor, y_factor.T, species_basis_matrix.T)


def solution(mesh):
    placed = (P(None, "gx", "gz", "gy"), P("gx", None), P("gy", None), P())
    return jax.shard_map(body, mesh=mesh, in_specs=placed, out_specs=P("gz", None), check_vma=False)
```

```python
import functools

import jax
import jax.numpy as jnp
from jax import lax
from jax.experimental import pallas as pl
from jax.experimental.pallas import tpu as pltpu
from jax.sharding import PartitionSpec as P

MESH = pl.DeviceIdType.MESH
F32 = jnp.float32
I32 = jnp.int32
BF16 = jnp.bfloat16
NT = (((1,), (1,)), ((), ()))

NGX, NGZ, NGY = 16, 8, 2
XL, ZL = 24, 48
RI, RJ, RP, NS = 48, 48, 4, 8
ZG, ZZ = 10, 5
TOP = 32000.0
BIAS = 124.0
SHARE = 6
CH = 4
ROWS = XL * ZL // CH
FAR = (4, 12, 3, 11, 5, 13, 2, 10, 6, 14, 1, 9, 7, 15, 8)


def rem(number, by):
    return lax.rem(number, I32(by))


def div(number, by):
    return lax.div(number, I32(by))


def encode(value, inverse):
    whole = jnp.round(value * inverse)
    size = jnp.abs(whole)
    high = jnp.floor(size * (1.0 / 128.0))
    code = jnp.exp2(high - BIAS) * (1.0 + (size - 128.0 * high) * (1.0 / 128.0))
    return jnp.where(whole < 0.0, -code, code)


def decode(code):
    size = jnp.abs(code)
    high = jnp.floor(jnp.log2(size) + 0.002)
    whole = jnp.round(128.0 * (high + (BIAS - 1.0) + size * jnp.exp2(-high)))
    return jnp.where(code < 0.0, -whole, whole)


def scale_of(largest):
    unit = (largest * (1.01 / TOP)).astype(BF16).astype(F32)
    return jnp.maximum(unit, 2.0**-100)


def split(value):
    high = value.astype(BF16)
    return high, (value - high.astype(F32)).astype(BF16)


def kernel(field, factors, out, fbuf, whi, wlo, mine, other, prt, tsum, xsend, xrecv, bd, asend, arecv,
           acc, d2, csend, owns, theirs, left_buf, right_buf, gsum, fin,
           f_sem, es_sem, er_sem, xs_sem, xr_sem, as_sem, ar_sem, cs_sem, cr_sem, gs_sem, gr_sem, qs_sem, qr_sem):
    gx, gz, gy = lax.axis_index("gx"), lax.axis_index("gz"), lax.axis_index("gy")
    y_lo, z_at = div(gx, 8), rem(gx, 8)
    quad = y_lo * 2 + gy
    x_at, y_hi = div(gz, 2), rem(gz, 2)

    def to_gx(dd):
        return {"gx": rem(gx + dd, NGX), "gz": gz, "gy": gy}

    def in_quad(dy, dc):
        return {"gx": rem(y_lo + dy, 2) * 8 + z_at, "gz": gz, "gy": rem(gy + dc, 2)}

    def quad_of(dy, dc):
        return rem(y_lo + dy, 2) * 2 + rem(gy + dc, 2)

    def charged(dx, dh):
        return {"gx": div(x_at, 2) * 8 + z_at, "gz": rem(x_at + dx, 4) * 2 + rem(y_hi + dh, 2), "gy": rem(x_at, 2)}

    loads = []
    for c in range(CH):
        part = pl.ds(c * (NS // CH), NS // CH)
        loads.append(pltpu.make_async_copy(field.at[part], fbuf.at[part], f_sem.at[c]))
        loads[-1].start()

    barrier = pltpu.get_barrier_semaphore()

    def greet(there):
        pl.semaphore_signal(barrier, inc=1, device_id=there, device_id_type=MESH)

    for dd in FAR[0:4]:
        greet(to_gx(dd))
    for b in range(2):
        @pl.when(2 * quad + b != gz)
        def _():
            for w in range(4):
                greet({"gx": w // 2 * 8 + z_at, "gz": 2 * quad + b, "gy": w % 2})

    for dd in FAR[4:]:
        greet(to_gx(dd))
    for dy in range(2):
        greet(in_quad(dy, 1))


    x32 = factors[RJ:RJ + XL, 0:RI]
    low = jnp.concatenate([x32[16:24], jnp.zeros((8, RI), F32)], axis=0)
    gap = jnp.zeros((16, 16), F32)
    xsend[...] = jnp.concatenate([x32[0:16], gap, low, gap], axis=1).astype(BF16)

    lane = lax.broadcasted_iota(jnp.int32, (RJ, 256), 1)
    q = lane & 7
    dest = (gx + ((lane >> 3) & 15)) & 15
    late = (q >= 3).astype(jnp.int32)
    jl = 3 * dest + q - 3 * late
    pick = (lax.broadcasted_iota(jnp.int32, (RJ, 256), 0) == jl) & (q < SHARE)
    spread = lax.dot_general(factors[0:RJ, :].astype(BF16), pick.astype(F32).astype(BF16), (((0,), (0,)), ((), ())), preferred_element_type=F32)
    plane = (2 * (((lane >> 7) + gy) & 1) + late)[0:1]
    basis = factors[RJ + XL:RJ + XL + RP, 0:NS]
    for s in range(NS):
        mix = jnp.zeros((1, 256), F32)
        for p in range(RP):
            mix = mix + jnp.where(plane == p, basis[p:p + 1, s:s + 1], 0.0)
        high, rest = split(spread * mix)
        whi[128 * s:128 * s + 128, :] = high
        wlo[128 * s:128 * s + 128, :] = rest

    spare = lax.broadcasted_iota(jnp.int32, (ROWS, 128), 1) & 7
    for load in loads:
        load.wait()
    left = jnp.concatenate([fbuf[s].reshape(XL * ZL, 128) for s in range(NS)], axis=1)
    part = jnp.dot(left, whi[...], preferred_element_type=F32) + jnp.dot(left, wlo[...], preferred_element_type=F32)
    mine[...] = part[:, 0:128]
    pl.semaphore_wait(barrier, NGX - 1 + 2 + NGZ - 1)
    exchanges = []
    for c in range(CH):
        span = pl.ds(c * ROWS, ROWS)
        away = part[c * ROWS:c * ROWS + ROWS, 128:256]
        unit = scale_of(jnp.max(jnp.abs(away), keepdims=True))
        other[span, :] = jnp.where(spare == SHARE, unit, encode(away, 1.0 / unit)).astype(BF16)
        exchanges.append(pltpu.make_async_remote_copy(
            other.at[span], prt.at[span], es_sem.at[c], er_sem.at[c], device_id=in_quad(0, 1), device_id_type=MESH))
        exchanges[-1].start()

    xcopies = [
        pltpu.make_async_remote_copy(xsend, xrecv.at[dd], xs_sem.at[dd], xr_sem.at[dd], device_id=to_gx(dd), device_id_type=MESH)
        for dd in FAR
    ]
    for copy in xcopies:
        copy.start()

    largest = jnp.zeros((8, 128), F32)
    for c in range(CH):
        exchanges[c].wait_recv()
        span = pl.ds(c * ROWS, ROWS)
        came = prt[span, :].astype(F32)
        total = mine[span, :] + jnp.where(spare < SHARE, decode(came) * came[0:1, SHARE:SHARE + 1], 0.0)
        tsum[span, :] = total
        largest = jnp.maximum(largest, jnp.max(jnp.abs(total).reshape(ROWS // 8, 8, 128), axis=0))
    unit = scale_of(jnp.max(largest, keepdims=True))
    inverse = 1.0 / unit

    line = lax.broadcasted_iota(jnp.int32, (NGX, 8, 128), 1)

    def coded(zg):
        pieces = []
        for zz in range(ZZ):
            z = zg + ZG * zz
            pieces.append(tsum[pl.ds(z, XL, stride=ZL), :] if z < ZL else jnp.zeros((XL, 128), F32))
        pieces.append(jnp.zeros((8, 128), F32))
        return encode(jnp.concatenate(pieces, axis=0).T, inverse).reshape(NGX, 8, 128)

    tails = (coded(8), coded(9))

    def packed(zg):
        if zg < 6:
            return jnp.where(line < SHARE, coded(zg), pltpu.roll(tails[zg // 3], 6 - 2 * (zg % 3), axis=1))
        return jnp.where(line == SHARE, unit.reshape(1, 1, 1), coded(zg))

    for m in range(4):
        asend[:, 16 * m:16 * m + 16, :] = jnp.concatenate([packed(2 * m), packed(2 * m + 1)], axis=1).astype(BF16)

    acopies = {
        dd: pltpu.make_async_remote_copy(asend.at[dd], arecv.at[dd], as_sem.at[dd], ar_sem.at[dd], device_id=to_gx(dd), device_id_type=MESH)
        for dd in range(1, NGX)
    }
    for dd in FAR:
        acopies[dd].start()

    for copy in xcopies:
        copy.wait_recv()
    xrecv[0] = xsend[...]
    row = lax.broadcasted_iota(jnp.int32, (128, 256), 0)
    lane = lax.broadcasted_iota(jnp.int32, (128, 256), 1)
    slot = jnp.zeros((128, 256), jnp.int32)
    for zz in range(1, ZZ):
        slot = slot + (lane >= RI * zz).astype(jnp.int32)
    want = lane - RI * slot
    first = ((row == want) & (lane < RI * ZZ)).astype(F32).astype(BF16)
    second = ((row == want + 64) & (lane < RI * ZZ)).astype(F32).astype(BF16)
    everything = xrecv[...].reshape(NGX * 16, 128)
    upper = jnp.dot(everything, first, preferred_element_type=F32)
    lower = jnp.dot(everything, second, preferred_element_type=F32)
    column = slot[0:XL]
    for dd in range(NGX):
        block = jnp.concatenate([upper[16 * dd:16 * dd + 16], lower[16 * dd:16 * dd + 8]], axis=0)
        stack = [jnp.where(column == zz, block, 0.0) for zz in range(ZZ)] + [jnp.zeros((8, 256), F32)]
        bd[128 * dd:128 * dd + 128, :] = jnp.concatenate(stack, axis=0).astype(BF16)

    eight = lax.broadcasted_iota(jnp.int32, (8, 128), 0)
    for k in range(NGX // 2):
        sides = []
        for dd in (2 * k, 2 * k + 1):
            if dd:
                acopies[dd].wait_recv()
            held = (arecv if dd else asend)[dd].astype(F32)
            value = decode(held) * held[48 + SHARE:48 + SHARE + 1, :]
            tails = []
            for t in range(2):
                a, b, c = (pltpu.roll(value[24 * t + 8 * n:24 * t + 8 * n + 8], 2 * n + 2, axis=0) for n in range(3))
                tails.append(jnp.where(eight < 2, a, jnp.where(eight < 4, b, c)))
            sides.append(jnp.concatenate([value] + tails, axis=0))
        high, rest = split(jnp.concatenate(sides, axis=1))
        product = jnp.dot(jnp.concatenate([high, rest], axis=0), bd[256 * k:256 * k + 256, :], preferred_element_type=F32)
        if k == 0:
            acc[...] = product
        else:
            acc[...] += product

    core = acc[0:80, :] + acc[80:160, :]
    for zz in range(ZZ):
        d2[80 * zz:80 * zz + 80, 0:RI] = core[:, RI * zz:RI * zz + RI]
    rows = jnp.concatenate([d2[pl.ds(c, ZL, stride=8), :][:, 0:RI] for c in range(SHARE)], axis=1)
    unit = scale_of(jnp.max(jnp.abs(rows), keepdims=True))
    words = encode(rows, 1.0 / unit)
    rest = [words[16 * k:16 * k + 16, 256:288] for k in range(3)] + [jnp.broadcast_to(unit, (16, 32))]
    csend[...] = jnp.concatenate([words[:, 0:128], words[:, 128:256], jnp.concatenate(rest, axis=1)], axis=0).astype(BF16)

    ccopies = []
    for dx, dh in ((2, 1), (1, 1), (3, 1), (0, 1), (2, 0), (1, 0), (3, 0)):
        k = 2 * dx + dh
        ccopies.append(pltpu.make_async_remote_copy(
            csend, theirs.at[4 * y_hi + quad], cs_sem.at[k], cr_sem.at[4 + 4 * y_hi + quad], device_id=charged(dx, dh), device_id_type=MESH))
    for dy, dc in ((1, 1), (1, 0), (0, 1)):
        ccopies.append(pltpu.make_async_remote_copy(
            csend, owns.at[quad], cs_sem.at[8 + 2 * dy + dc], cr_sem.at[quad], device_id=in_quad(dy, dc), device_id_type=MESH))
    for copy in ccopies:
        copy.start()
    for copy in xcopies + exchanges + list(acopies.values()):
        copy.wait_send()
    owns[quad] = csend[...]

    def opened(pieces, buf, at, low):
        rests = []
        for w in range(4):
            held = pieces[w].astype(F32)
            value = decode(held) * held[96:97, 96:97]
            for k in range(2):
                lanes = pl.ds(256 * w + 128 * k, 128)
                buf[pl.ds(at, ZL), lanes], buf[pl.ds(low, ZL), lanes] = split(value[ZL * k:ZL * k + ZL])
            rests.append(jnp.concatenate([value[96:112, 32 * k:32 * k + 32] for k in range(3)], axis=0))
        buf[pl.ds(at, ZL), 1024:1152], buf[pl.ds(low, ZL), 1024:1152] = split(jnp.concatenate(rests, axis=1))

    for dy, dc in ((0, 1), (1, 0), (1, 1)):
        w = quad_of(dy, dc)
        pltpu.make_async_copy(owns.at[w], owns.at[w], cr_sem.at[w]).wait()
    opened([owns[w] for w in range(4)], left_buf, 0, ZL)
    for near in range(2):
        b = rem(y_hi + near, 2)

        @pl.when(2 * quad + b != gz)
        def _():
            for w in range(4):
                k = 4 * b + w
                pltpu.make_async_copy(theirs.at[k], theirs.at[k], cr_sem.at[4 + k]).wait()

        @pl.when(2 * quad + b == gz)
        def _():
            for w in range(4):
                theirs[4 * b + w] = owns[w]

        at = pl.multiple_of(ZL * b, 16)
        opened([theirs[4 * b + w] for w in range(4)], right_buf, at, at + 128)
    right_buf[96:128, :] = jnp.zeros((32, 1152), BF16)
    right_buf[224:256, :] = jnp.zeros((32, 1152), BF16)
    gram = lax.dot_general(left_buf[...], right_buf[...], NT, preferred_element_type=F32)
    gram = (gram[0:ZL] + gram[ZL:2 * ZL]) * (1.0 / (RI * RJ * RP))
    gram = gram[:, 0:128] + gram[:, 128:256]
    unit = scale_of(jnp.max(jnp.abs(gram), keepdims=True))
    beyond = lax.broadcasted_iota(jnp.int32, (ZL, 128), 1) >= 96
    gsum[z_at] = jnp.where(beyond, unit, encode(gram, 1.0 / unit)).astype(BF16)

    gcopies = [
        pltpu.make_async_remote_copy(
            gsum.at[z_at], gsum.at[z_at], gs_sem.at[dz], gr_sem.at[z_at],
            device_id={"gx": y_lo * 8 + rem(z_at + dz, 8), "gz": gz, "gy": gy}, device_id_type=MESH)
        for dz in (4, 3, 5, 2, 6, 1, 7)
    ]
    for copy in gcopies:
        copy.start()
    for copy in ccopies:
        copy.wait_send()
    for dz in (7, 1, 6, 2, 5, 3, 4):
        w = rem(z_at + dz, 8)
        pltpu.make_async_copy(gsum.at[w], gsum.at[w], gr_sem.at[w]).wait()
    total = jnp.zeros((ZL, 128), F32)
    for k in range(8):
        held = gsum[k].astype(F32)
        total = total + decode(held) * held[:, 96:97]
    fin[quad] = total

    qcopies = [
        pltpu.make_async_remote_copy(
            fin.at[quad], fin.at[quad], qs_sem.at[2 * dy + dc], qr_sem.at[quad], device_id=in_quad(dy, dc), device_id_type=MESH)
        for dy, dc in ((1, 1), (1, 0), (0, 1))
    ]
    for copy in qcopies:
        copy.start()
    for copy in gcopies:
        copy.wait_send()
    for dy, dc in ((0, 1), (1, 0), (1, 1)):
        w = quad_of(dy, dc)
        pltpu.make_async_copy(fin.at[w], fin.at[w], qr_sem.at[w]).wait()
    out[...] = jnp.concatenate([fin[w][:, 0:96] for w in range(4)], axis=1)

    for copy in qcopies:
        copy.wait_send()


def body(field, x_factor, y_factor, species_basis_matrix):
    vmem = pl.BlockSpec(memory_space=pltpu.VMEM)
    dma = pltpu.SemaphoreType.DMA
    factors = (
        jnp.pad(y_factor.T.astype(F32), ((0, XL + 8), (0, 0)))
        + jnp.pad(x_factor.astype(F32), ((RJ, 8), (0, 128 - RI)))
        + jnp.pad(species_basis_matrix.T, ((RJ + XL, 8 - RP), (0, 128 - NS)))
    )
    return pl.pallas_call(
        kernel,
        out_shape=jax.ShapeDtypeStruct((ZL, NGZ * ZL), F32),
        in_specs=[pl.BlockSpec(memory_space=pltpu.HBM), vmem],
        out_specs=vmem,
        scratch_shapes=[
            pltpu.VMEM((NS, XL, ZL, 128), BF16),
            pltpu.VMEM((1024, 256), BF16),
            pltpu.VMEM((1024, 256), BF16),
            pltpu.VMEM((XL * ZL, 128), F32),
            pltpu.VMEM((XL * ZL, 128), BF16),
            pltpu.VMEM((XL * ZL, 128), BF16),
            pltpu.VMEM((XL * ZL, 128), F32),
            pltpu.VMEM((16, 128), BF16),
            pltpu.VMEM((NGX, 16, 128), BF16),
            pltpu.VMEM((NGX * 128, 256), BF16),
            pltpu.VMEM((NGX, 64, 128), BF16),
            pltpu.VMEM((NGX, 64, 128), BF16),
            pltpu.VMEM((160, 256), F32),
            pltpu.VMEM((400, 128), F32),
            pltpu.VMEM((112, 128), BF16),
            pltpu.VMEM((4, 112, 128), BF16),
            pltpu.VMEM((8, 112, 128), BF16),
            pltpu.VMEM((96, 1152), BF16),
            pltpu.VMEM((256, 1152), BF16),
            pltpu.VMEM((8, ZL, 128), BF16),
            pltpu.VMEM((4, ZL, 128), F32),
            dma((CH,)), dma((CH,)), dma((CH,)), dma((NGX,)), dma((NGX,)), dma((NGX,)), dma((NGX,)),
            dma((12,)), dma((12,)), dma((8,)), dma((8,)), dma((4,)), dma((4,)),
        ],
        compiler_params=pltpu.CompilerParams(collective_id=0, has_side_effects=True, vmem_limit_bytes=53 * 1024 * 1024),
    )(field, factors)


def solution(mesh):
    placed = (P(None, "gx", "gz", "gy"), P("gx", None), P("gy", None), P())
    return jax.shard_map(body, mesh=mesh, in_specs=placed, out_specs=P("gz", None), check_vma=False)
```

```python
import functools

import jax
import jax.numpy as jnp
from jax import lax
from jax.experimental import pallas as pl
from jax.experimental.pallas import tpu as pltpu
from jax.sharding import PartitionSpec as P

MESH = pl.DeviceIdType.MESH
F32 = jnp.float32
I32 = jnp.int32
BF16 = jnp.bfloat16
NT = (((1,), (1,)), ((), ()))

NGX, NGZ, NGY = 16, 8, 2
XL, ZL = 24, 48
RI, RJ, RP, NS = 48, 48, 4, 8
ZG, ZZ = 10, 5
TOP = 32000.0
BIAS = 124.0
SHARE = 6
CH = 4
FAR = (4, 12, 3, 11, 5, 13, 2, 10, 6, 14, 1, 9, 7, 15, 8)
PLACES = FAR + (0,)


def rem(number, by):
    return lax.rem(number, I32(by))


def div(number, by):
    return lax.div(number, I32(by))


def encode(value, inverse):
    whole = jnp.round(value * inverse)
    size = jnp.abs(whole)
    high = jnp.floor(size * (1.0 / 128.0))
    code = jnp.exp2(high - BIAS) * (1.0 + (size - 128.0 * high) * (1.0 / 128.0))
    return jnp.where(whole < 0.0, -code, code)


def decode(code):
    size = jnp.abs(code)
    high = jnp.floor(jnp.log2(size) + 0.002)
    whole = jnp.round(128.0 * (high + (BIAS - 1.0) + size * jnp.exp2(-high)))
    return jnp.where(code < 0.0, -whole, whole)


def scale_of(largest):
    unit = (largest * (1.01 / TOP)).astype(BF16).astype(F32)
    return jnp.maximum(unit, 2.0**-100)


def split(value):
    high = value.astype(BF16)
    return high, (value - high.astype(F32)).astype(BF16)


def kernel(field, factors, out, fbuf, whi, wlo, mine, away, packed, other, prt, xsend, xrecv, bd, asend, arecv,
           acc, d2, csend, owns, theirs, left_buf, right_buf, gsum, fin,
           f_sem, es_sem, er_sem, xs_sem, xr_sem, as_sem, ar_sem, cs_sem, cr_sem, gs_sem, gr_sem, qs_sem, qr_sem):
    gx, gz, gy = lax.axis_index("gx"), lax.axis_index("gz"), lax.axis_index("gy")
    y_lo, z_at = div(gx, 8), rem(gx, 8)
    quad = y_lo * 2 + gy
    x_at, y_hi = div(gz, 2), rem(gz, 2)

    def to_gx(dd):
        return {"gx": rem(gx + dd, NGX), "gz": gz, "gy": gy}

    def in_quad(dy, dc):
        return {"gx": rem(y_lo + dy, 2) * 8 + z_at, "gz": gz, "gy": rem(gy + dc, 2)}

    def quad_of(dy, dc):
        return rem(y_lo + dy, 2) * 2 + rem(gy + dc, 2)

    def charged(dx, dh):
        return {"gx": div(x_at, 2) * 8 + z_at, "gz": rem(x_at + dx, 4) * 2 + rem(y_hi + dh, 2), "gy": rem(x_at, 2)}

    loads = []
    for c in range(CH):
        part = pl.ds(c * (NS // CH), NS // CH)
        loads.append(pltpu.make_async_copy(field.at[part], fbuf.at[part], f_sem.at[c]))
        loads[-1].start()

    barrier = pltpu.get_barrier_semaphore()

    def greet(there):
        pl.semaphore_signal(barrier, inc=1, device_id=there, device_id_type=MESH)

    for dd in FAR[0:4]:
        greet(to_gx(dd))
    for b in range(2):
        @pl.when(2 * quad + b != gz)
        def _():
            for w in range(4):
                greet({"gx": w // 2 * 8 + z_at, "gz": 2 * quad + b, "gy": w % 2})

    for dd in FAR[4:]:
        greet(to_gx(dd))
    for dy in range(2):
        greet(in_quad(dy, 1))


    x32 = factors[RJ:RJ + XL, 0:RI]
    low = jnp.concatenate([x32[16:24], jnp.zeros((8, RI), F32)], axis=0)
    gap = jnp.zeros((16, 16), F32)
    xsend[...] = jnp.concatenate([x32[0:16], gap, low, gap], axis=1).astype(BF16)

    lane = lax.broadcasted_iota(jnp.int32, (RJ, 256), 1)
    q = lane & 7
    place = (lane >> 3) & 15
    dest = gx + jnp.zeros((RJ, 256), jnp.int32)
    for n, dd in enumerate(PLACES):
        dest = dest + jnp.where(place == n, dd, 0)
    dest = dest & 15
    late = (q >= 3).astype(jnp.int32)
    jl = 3 * dest + q - 3 * late
    pick = (lax.broadcasted_iota(jnp.int32, (RJ, 256), 0) == jl) & (q < SHARE)
    spread = lax.dot_general(factors[0:RJ, :].astype(BF16), pick.astype(F32).astype(BF16), (((0,), (0,)), ((), ())), preferred_element_type=F32)
    plane = (2 * (((lane >> 7) + gy) & 1) + late)[0:1]
    basis = factors[RJ + XL:RJ + XL + RP, 0:NS]
    for s in range(NS):
        mix = jnp.zeros((1, 256), F32)
        for p in range(RP):
            mix = mix + jnp.where(plane == p, basis[p:p + 1, s:s + 1], 0.0)
        high, rest = split(spread * mix)
        whi[128 * s:128 * s + 128, :] = high
        wlo[128 * s:128 * s + 128, :] = rest

    for load in loads:
        load.wait()
    left = jnp.concatenate([fbuf[s].reshape(XL * ZL, 128) for s in range(NS)], axis=1)
    part = jnp.dot(left, whi[...], preferred_element_type=F32) + jnp.dot(left, wlo[...], preferred_element_type=F32)
    mine[...] = part[:, 0:128]
    away[...] = part[:, 128:256]
    largest = jnp.max(jnp.abs(part[:, 0:128]), keepdims=True)
    unit = scale_of(jnp.max(jnp.abs(part[:, 128:256]), keepdims=True))
    inverse = 1.0 / unit

    line = lax.broadcasted_iota(jnp.int32, (NGX, 8, 128), 1)
    scale_row = lax.broadcasted_iota(jnp.int32, (4, 64, 128), 1) == 48 + SHARE

    def tile(rows, zg):
        pieces = []
        for zz in range(ZZ):
            z = zg + ZG * zz
            pieces.append(rows[pl.ds(z, XL, stride=ZL), :] if z < ZL else jnp.zeros((XL, 128), F32))
        pieces.append(jnp.zeros((8, 128), F32))
        return jnp.concatenate(pieces, axis=0).T.reshape(NGX, 8, 128)

    def pairs(rows):
        tails = (tile(rows, 8), tile(rows, 9))
        for m in range(4):
            both = []
            for zg in (2 * m, 2 * m + 1):
                one = tile(rows, zg)
                both.append(jnp.where(line < SHARE, one, pltpu.roll(tails[zg // 3], 6 - 2 * (zg % 3), axis=1)) if zg < 6 else one)
            yield pl.ds(16 * m, 16), both

    for at, (a, b) in pairs(away):
        a, b = encode(a, inverse), encode(b, inverse)
        if at.start == 48:
            a = jnp.where(line == SHARE, unit.reshape(1, 1, 1), a)
        other[:, at, :] = jnp.concatenate([a, b], axis=1).astype(BF16)
    for at, both in pairs(mine):
        packed[:, at, :] = jnp.concatenate(both, axis=1)

    pl.semaphore_wait(barrier, NGX - 1 + 2 + NGZ - 1)
    exchanges = []
    for c in range(4):
        group = pl.ds(4 * c, 4)
        exchanges.append(pltpu.make_async_remote_copy(
            other.at[group], prt.at[group], es_sem.at[c], er_sem.at[c], device_id=in_quad(0, 1), device_id_type=MESH))
        exchanges[-1].start()
    xcopies = [
        pltpu.make_async_remote_copy(xsend, xrecv.at[dd], xs_sem.at[dd], xr_sem.at[dd], device_id=to_gx(dd), device_id_type=MESH)
        for dd in FAR
    ]
    for copy in xcopies:
        copy.start()

    acopies = {}
    for c in range(4):
        exchanges[c].wait_recv()
        group = pl.ds(4 * c, 4)
        came = prt[group].astype(F32)
        if c == 0:
            theirs_unit = came[0, 48 + SHARE:48 + SHARE + 1, 0:1]
            unit = scale_of(largest + theirs_unit * TOP)
            inverse = 1.0 / unit
        total = packed[group] + decode(came) * theirs_unit.reshape(1, 1, 1)
        asend[group] = jnp.where(scale_row, unit.reshape(1, 1, 1), encode(total, inverse)).astype(BF16)
        for n in range(4 * c, 4 * c + 4):
            dd = PLACES[n]
            if dd:
                acopies[dd] = pltpu.make_async_remote_copy(
                    asend.at[n], arecv.at[n], as_sem.at[dd], ar_sem.at[dd], device_id=to_gx(dd), device_id_type=MESH)
                acopies[dd].start()

    for copy in xcopies:
        copy.wait_recv()
    xrecv[0] = xsend[...]
    row = lax.broadcasted_iota(jnp.int32, (128, 256), 0)
    lane = lax.broadcasted_iota(jnp.int32, (128, 256), 1)
    slot = jnp.zeros((128, 256), jnp.int32)
    for zz in range(1, ZZ):
        slot = slot + (lane >= RI * zz).astype(jnp.int32)
    want = lane - RI * slot
    first = ((row == want) & (lane < RI * ZZ)).astype(F32).astype(BF16)
    second = ((row == want + 64) & (lane < RI * ZZ)).astype(F32).astype(BF16)
    everything = xrecv[...].reshape(NGX * 16, 128)
    upper = jnp.dot(everything, first, preferred_element_type=F32)
    lower = jnp.dot(everything, second, preferred_element_type=F32)
    column = slot[0:XL]
    for n, dd in enumerate((0,) + FAR):
        block = jnp.concatenate([upper[16 * dd:16 * dd + 16], lower[16 * dd:16 * dd + 8]], axis=0)
        stack = [jnp.where(column == zz, block, 0.0) for zz in range(ZZ)] + [jnp.zeros((8, 256), F32)]
        bd[128 * n:128 * n + 128, :] = jnp.concatenate(stack, axis=0).astype(BF16)

    eight = lax.broadcasted_iota(jnp.int32, (8, 128), 0)
    for k in range(NGX // 2):
        sides = []
        for dd in ((0,) + FAR)[2 * k:2 * k + 2]:
            if dd:
                acopies[dd].wait_recv()
            held = (arecv if dd else asend)[PLACES.index(dd)].astype(F32)
            value = decode(held) * held[48 + SHARE:48 + SHARE + 1, :]
            tails = []
            for t in range(2):
                a, b, c = (pltpu.roll(value[24 * t + 8 * n:24 * t + 8 * n + 8], 2 * n + 2, axis=0) for n in range(3))
                tails.append(jnp.where(eight < 2, a, jnp.where(eight < 4, b, c)))
            sides.append(jnp.concatenate([value] + tails, axis=0))
        high, rest = split(jnp.concatenate(sides, axis=1))
        product = jnp.dot(jnp.concatenate([high, rest], axis=0), bd[256 * k:256 * k + 256, :], preferred_element_type=F32)
        if k == 0:
            acc[...] = product
        else:
            acc[...] += product

    core = acc[0:80, :] + acc[80:160, :]
    for zz in range(ZZ):
        d2[80 * zz:80 * zz + 80, 0:RI] = core[:, RI * zz:RI * zz + RI]
    rows = jnp.concatenate([d2[pl.ds(c, ZL, stride=8), :][:, 0:RI] for c in range(SHARE)], axis=1)
    unit = scale_of(jnp.max(jnp.abs(rows), keepdims=True))
    words = encode(rows, 1.0 / unit)
    rest = [words[16 * k:16 * k + 16, 256:288] for k in range(3)] + [jnp.broadcast_to(unit, (16, 32))]
    csend[...] = jnp.concatenate([words[:, 0:128], words[:, 128:256], jnp.concatenate(rest, axis=1)], axis=0).astype(BF16)

    ccopies = []
    for dx, dh in ((2, 1), (1, 1), (3, 1), (0, 1), (2, 0), (1, 0), (3, 0)):
        k = 2 * dx + dh
        ccopies.append(pltpu.make_async_remote_copy(
            csend, theirs.at[4 * y_hi + quad], cs_sem.at[k], cr_sem.at[4 + 4 * y_hi + quad], device_id=charged(dx, dh), device_id_type=MESH))
    for dy, dc in ((1, 1), (1, 0), (0, 1)):
        ccopies.append(pltpu.make_async_remote_copy(
            csend, owns.at[quad], cs_sem.at[8 + 2 * dy + dc], cr_sem.at[quad], device_id=in_quad(dy, dc), device_id_type=MESH))
    for copy in ccopies:
        copy.start()
    for copy in xcopies + exchanges + list(acopies.values()):
        copy.wait_send()
    owns[quad] = csend[...]

    def opened(pieces, buf, at, low):
        rests = []
        for w in range(4):
            held = pieces[w].astype(F32)
            value = decode(held) * held[96:97, 96:97]
            for k in range(2):
                lanes = pl.ds(256 * w + 128 * k, 128)
                buf[pl.ds(at, ZL), lanes], buf[pl.ds(low, ZL), lanes] = split(value[ZL * k:ZL * k + ZL])
            rests.append(jnp.concatenate([value[96:112, 32 * k:32 * k + 32] for k in range(3)], axis=0))
        buf[pl.ds(at, ZL), 1024:1152], buf[pl.ds(low, ZL), 1024:1152] = split(jnp.concatenate(rests, axis=1))

    for dy, dc in ((0, 1), (1, 0), (1, 1)):
        w = quad_of(dy, dc)
        pltpu.make_async_copy(owns.at[w], owns.at[w], cr_sem.at[w]).wait()
    opened([owns[w] for w in range(4)], left_buf, 0, ZL)
    for near in range(2):
        b = rem(y_hi + near, 2)

        @pl.when(2 * quad + b != gz)
        def _():
            for w in range(4):
                k = 4 * b + w
                pltpu.make_async_copy(theirs.at[k], theirs.at[k], cr_sem.at[4 + k]).wait()

        @pl.when(2 * quad + b == gz)
        def _():
            for w in range(4):
                theirs[4 * b + w] = owns[w]

        at = pl.multiple_of(ZL * b, 16)
        opened([theirs[4 * b + w] for w in range(4)], right_buf, at, at + 128)
    right_buf[96:128, :] = jnp.zeros((32, 1152), BF16)
    right_buf[224:256, :] = jnp.zeros((32, 1152), BF16)
    gram = lax.dot_general(left_buf[...], right_buf[...], NT, preferred_element_type=F32)
    gram = (gram[0:ZL] + gram[ZL:2 * ZL]) * (1.0 / (RI * RJ * RP))
    gram = gram[:, 0:128] + gram[:, 128:256]
    unit = scale_of(jnp.max(jnp.abs(gram), keepdims=True))
    beyond = lax.broadcasted_iota(jnp.int32, (ZL, 128), 1) >= 96
    gsum[z_at] = jnp.where(beyond, unit, encode(gram, 1.0 / unit)).astype(BF16)

    gcopies = [
        pltpu.make_async_remote_copy(
            gsum.at[z_at], gsum.at[z_at], gs_sem.at[dz], gr_sem.at[z_at],
            device_id={"gx": y_lo * 8 + rem(z_at + dz, 8), "gz": gz, "gy": gy}, device_id_type=MESH)
        for dz in (4, 3, 5, 2, 6, 1, 7)
    ]
    for copy in gcopies:
        copy.start()
    for copy in ccopies:
        copy.wait_send()
    for dz in (7, 1, 6, 2, 5, 3, 4):
        w = rem(z_at + dz, 8)
        pltpu.make_async_copy(gsum.at[w], gsum.at[w], gr_sem.at[w]).wait()
    total = jnp.zeros((ZL, 128), F32)
    for k in range(8):
        held = gsum[k].astype(F32)
        total = total + decode(held) * held[:, 96:97]
    fin[quad] = total

    qcopies = [
        pltpu.make_async_remote_copy(
            fin.at[quad], fin.at[quad], qs_sem.at[2 * dy + dc], qr_sem.at[quad], device_id=in_quad(dy, dc), device_id_type=MESH)
        for dy, dc in ((1, 1), (1, 0), (0, 1))
    ]
    for copy in qcopies:
        copy.start()
    for copy in gcopies:
        copy.wait_send()
    for dy, dc in ((0, 1), (1, 0), (1, 1)):
        w = quad_of(dy, dc)
        pltpu.make_async_copy(fin.at[w], fin.at[w], qr_sem.at[w]).wait()
    out[...] = jnp.concatenate([fin[w][:, 0:96] for w in range(4)], axis=1)

    for copy in qcopies:
        copy.wait_send()


def body(field, x_factor, y_factor, species_basis_matrix):
    vmem = pl.BlockSpec(memory_space=pltpu.VMEM)
    dma = pltpu.SemaphoreType.DMA
    factors = (
        jnp.pad(y_factor.T.astype(F32), ((0, XL + 8), (0, 0)))
        + jnp.pad(x_factor.astype(F32), ((RJ, 8), (0, 128 - RI)))
        + jnp.pad(species_basis_matrix.T, ((RJ + XL, 8 - RP), (0, 128 - NS)))
    )
    return pl.pallas_call(
        kernel,
        out_shape=jax.ShapeDtypeStruct((ZL, NGZ * ZL), F32),
        in_specs=[pl.BlockSpec(memory_space=pltpu.HBM), vmem],
        out_specs=vmem,
        scratch_shapes=[
            pltpu.VMEM((NS, XL, ZL, 128), BF16),
            pltpu.VMEM((1024, 256), BF16),
            pltpu.VMEM((1024, 256), BF16),
            pltpu.VMEM((XL * ZL, 128), F32),
            pltpu.VMEM((XL * ZL, 128), F32),
            pltpu.VMEM((NGX, 64, 128), F32),
            pltpu.VMEM((NGX, 64, 128), BF16),
            pltpu.VMEM((NGX, 64, 128), BF16),
            pltpu.VMEM((16, 128), BF16),
            pltpu.VMEM((NGX, 16, 128), BF16),
            pltpu.VMEM((NGX * 128, 256), BF16),
            pltpu.VMEM((NGX, 64, 128), BF16),
            pltpu.VMEM((NGX, 64, 128), BF16),
            pltpu.VMEM((160, 256), F32),
            pltpu.VMEM((400, 128), F32),
            pltpu.VMEM((112, 128), BF16),
            pltpu.VMEM((4, 112, 128), BF16),
            pltpu.VMEM((8, 112, 128), BF16),
            pltpu.VMEM((96, 1152), BF16),
            pltpu.VMEM((256, 1152), BF16),
            pltpu.VMEM((8, ZL, 128), BF16),
            pltpu.VMEM((4, ZL, 128), F32),
            dma((CH,)), dma((CH,)), dma((CH,)), dma((NGX,)), dma((NGX,)), dma((NGX,)), dma((NGX,)),
            dma((12,)), dma((12,)), dma((8,)), dma((8,)), dma((4,)), dma((4,)),
        ],
        compiler_params=pltpu.CompilerParams(collective_id=0, has_side_effects=True, vmem_limit_bytes=53 * 1024 * 1024),
    )(field, factors)


def solution(mesh):
    placed = (P(None, "gx", "gz", "gy"), P("gx", None), P("gy", None), P())
    return jax.shard_map(body, mesh=mesh, in_specs=placed, out_specs=P("gz", None), check_vma=False)
```

```python
import functools

import jax
import jax.numpy as jnp
from jax import lax
from jax.experimental import pallas as pl
from jax.experimental.pallas import tpu as pltpu
from jax.sharding import PartitionSpec as P

MESH = pl.DeviceIdType.MESH
F32 = jnp.float32
I32 = jnp.int32
BF16 = jnp.bfloat16
NT = (((1,), (1,)), ((), ()))

NGX, NGZ, NGY = 16, 8, 2
XL, ZL = 24, 48
RI, RJ, RP, NS = 48, 48, 4, 8
ZG, ZZ = 10, 5
TOP = 32000.0
BIAS = 124.0
SHARE = 6
CH = 4
FAR = (4, 12, 3, 11, 5, 13, 2, 10, 6, 14, 1, 9, 7, 15, 8)
PLACES = FAR + (0,)


def rem(number, by):
    return lax.rem(number, I32(by))


def div(number, by):
    return lax.div(number, I32(by))


def encode(value, inverse):
    whole = jnp.round(value * inverse)
    size = jnp.abs(whole)
    high = jnp.floor(size * (1.0 / 128.0))
    code = jnp.exp2(high - BIAS) * (1.0 + (size - 128.0 * high) * (1.0 / 128.0))
    return jnp.where(whole < 0.0, -code, code)


def decode(code):
    size = jnp.abs(code)
    high = jnp.floor(jnp.log2(size) + 0.002)
    whole = jnp.round(128.0 * (high + (BIAS - 1.0) + size * jnp.exp2(-high)))
    return jnp.where(code < 0.0, -whole, whole)


def scale_of(largest):
    unit = (largest * (1.01 / TOP)).astype(BF16).astype(F32)
    return jnp.maximum(unit, 2.0**-100)


def split(value):
    high = value.astype(BF16)
    return high, (value - high.astype(F32)).astype(BF16)


def kernel(field, factors, out, fbuf, whi, wlo, mine, away, packed, other, prt, xsend, xrecv, bd, asend, arecv,
           acc, d2, csend, owns, theirs, left_buf, right_buf, gsum, fin,
           f_sem, es_sem, er_sem, xs_sem, xr_sem, as_sem, ar_sem, cs_sem, cr_sem, gs_sem, gr_sem, qs_sem, qr_sem):
    gx, gz, gy = lax.axis_index("gx"), lax.axis_index("gz"), lax.axis_index("gy")
    y_lo, z_at = div(gx, 8), rem(gx, 8)
    quad = y_lo * 2 + gy
    x_at, y_hi = div(gz, 2), rem(gz, 2)

    def to_gx(dd):
        return {"gx": rem(gx + dd, NGX), "gz": gz, "gy": gy}

    def in_quad(dy, dc):
        return {"gx": rem(y_lo + dy, 2) * 8 + z_at, "gz": gz, "gy": rem(gy + dc, 2)}

    def quad_of(dy, dc):
        return rem(y_lo + dy, 2) * 2 + rem(gy + dc, 2)

    def charged(dx, dh):
        return {"gx": div(x_at, 2) * 8 + z_at, "gz": rem(x_at + dx, 4) * 2 + rem(y_hi + dh, 2), "gy": rem(x_at, 2)}

    loads = []
    for c in range(CH):
        part = pl.ds(c * (NS // CH), NS // CH)
        loads.append(pltpu.make_async_copy(field.at[part], fbuf.at[part], f_sem.at[c]))
        loads[-1].start()

    barrier = pltpu.get_barrier_semaphore()

    def greet(there):
        pl.semaphore_signal(barrier, inc=1, device_id=there, device_id_type=MESH)

    for dd in FAR[0:4]:
        greet(to_gx(dd))
    for b in range(2):
        @pl.when(2 * quad + b != gz)
        def _():
            for w in range(4):
                greet({"gx": w // 2 * 8 + z_at, "gz": 2 * quad + b, "gy": w % 2})

    for dd in FAR[4:]:
        greet(to_gx(dd))
    for dy in range(2):
        greet(in_quad(dy, 1))


    x32 = factors[RJ:RJ + XL, 0:RI]
    low = jnp.concatenate([x32[16:24], jnp.zeros((8, RI), F32)], axis=0)
    gap = jnp.zeros((16, 16), F32)
    xsend[...] = jnp.concatenate([x32[0:16], gap, low, gap], axis=1).astype(BF16)

    lane = lax.broadcasted_iota(jnp.int32, (RJ, 256), 1)
    q = lane & 7
    place = (lane >> 3) & 15
    dest = gx + jnp.zeros((RJ, 256), jnp.int32)
    for n, dd in enumerate(PLACES):
        dest = dest + jnp.where(place == n, dd, 0)
    dest = dest & 15
    late = (q >= 3).astype(jnp.int32)
    jl = 3 * dest + q - 3 * late
    pick = (lax.broadcasted_iota(jnp.int32, (RJ, 256), 0) == jl) & (q < SHARE)
    spread = lax.dot_general(factors[0:RJ, :].astype(BF16), pick.astype(F32).astype(BF16), (((0,), (0,)), ((), ())), preferred_element_type=F32)
    plane = (2 * (((lane >> 7) + gy) & 1) + late)[0:1]
    basis = factors[RJ + XL:RJ + XL + RP, 0:NS]
    for s in range(NS):
        mix = jnp.zeros((1, 256), F32)
        for p in range(RP):
            mix = mix + jnp.where(plane == p, basis[p:p + 1, s:s + 1], 0.0)
        high, rest = split(spread * mix)
        whi[128 * s:128 * s + 128, :] = high
        wlo[128 * s:128 * s + 128, :] = rest

    for load in loads:
        load.wait()
    left = jnp.concatenate([fbuf[s].reshape(XL * ZL, 128) for s in range(NS)], axis=1)
    part = jnp.dot(left, whi[...], preferred_element_type=F32) + jnp.dot(left, wlo[...], preferred_element_type=F32)
    mine[0:XL * ZL, :] = part[:, 0:128]
    away[0:XL * ZL, :] = part[:, 128:256]
    largest = jnp.max(jnp.abs(part[:, 0:128]), keepdims=True)
    unit = scale_of(jnp.max(jnp.abs(part[:, 128:256]), keepdims=True))
    inverse = 1.0 / unit

    line = lax.broadcasted_iota(jnp.int32, (NGX, 8, 128), 1)
    scale_row = lax.broadcasted_iota(jnp.int32, (4, 64, 128), 1) == 48 + SHARE

    def tile(rows, zg):
        pieces = []
        for zz in range(ZZ):
            z = zg + ZG * zz
            pieces.append(rows[pl.ds(z, XL, stride=ZL), :] if z < ZL else jnp.zeros((XL, 128), F32))
        pieces.append(jnp.zeros((8, 128), F32))
        return jnp.concatenate(pieces, axis=0).T.reshape(NGX, 8, 128)

    def pairs(rows):
        tails = (tile(rows, 8), tile(rows, 9))
        for m in range(4):
            both = []
            for zg in (2 * m, 2 * m + 1):
                one = tile(rows, zg)
                both.append(jnp.where(line < SHARE, one, pltpu.roll(tails[zg // 3], 6 - 2 * (zg % 3), axis=1)) if zg < 6 else one)
            yield pl.ds(16 * m, 16), both

    for at, (a, b) in pairs(away):
        a, b = encode(a, inverse), encode(b, inverse)
        if at.start == 48:
            a = jnp.where(line == SHARE, unit.reshape(1, 1, 1), a)
        other[:, at, :] = jnp.concatenate([a, b], axis=1).astype(BF16)
    for at, both in pairs(mine):
        packed[:, at, :] = jnp.concatenate(both, axis=1)

    pl.semaphore_wait(barrier, NGX - 1 + 2 + NGZ - 1)
    exchanges = []
    for c in range(4):
        group = pl.ds(4 * c, 4)
        exchanges.append(pltpu.make_async_remote_copy(
            other.at[group], prt.at[group], es_sem.at[c], er_sem.at[c], device_id=in_quad(0, 1), device_id_type=MESH))
        exchanges[-1].start()
    xcopies = [
        pltpu.make_async_remote_copy(xsend, xrecv.at[dd], xs_sem.at[dd], xr_sem.at[dd], device_id=to_gx(dd), device_id_type=MESH)
        for dd in FAR
    ]
    for copy in xcopies:
        copy.start()

    acopies = {}
    for c in range(4):
        exchanges[c].wait_recv()
        group = pl.ds(4 * c, 4)
        came = prt[group].astype(F32)
        if c == 0:
            theirs_unit = came[0, 48 + SHARE:48 + SHARE + 1, 0:1]
            unit = scale_of(largest + theirs_unit * TOP)
            inverse = 1.0 / unit
        total = packed[group] + decode(came) * theirs_unit.reshape(1, 1, 1)
        asend[group] = jnp.where(scale_row, unit.reshape(1, 1, 1), encode(total, inverse)).astype(BF16)
        for n in range(4 * c, 4 * c + 4):
            dd = PLACES[n]
            if dd:
                acopies[dd] = pltpu.make_async_remote_copy(
                    asend.at[n], arecv.at[n], as_sem.at[dd], ar_sem.at[dd], device_id=to_gx(dd), device_id_type=MESH)
                acopies[dd].start()

    for copy in xcopies:
        copy.wait_recv()
    xrecv[0] = xsend[...]
    row = lax.broadcasted_iota(jnp.int32, (128, 256), 0)
    lane = lax.broadcasted_iota(jnp.int32, (128, 256), 1)
    slot = jnp.zeros((128, 256), jnp.int32)
    for zz in range(1, ZZ):
        slot = slot + (lane >= RI * zz).astype(jnp.int32)
    want = lane - RI * slot
    first = ((row == want) & (lane < RI * ZZ)).astype(F32).astype(BF16)
    second = ((row == want + 64) & (lane < RI * ZZ)).astype(F32).astype(BF16)
    everything = xrecv[...].reshape(NGX * 16, 128)
    upper = jnp.dot(everything, first, preferred_element_type=F32)
    lower = jnp.dot(everything, second, preferred_element_type=F32)
    column = slot[0:XL]
    for n, dd in enumerate((0,) + FAR):
        block = jnp.concatenate([upper[16 * dd:16 * dd + 16], lower[16 * dd:16 * dd + 8]], axis=0)
        stack = [jnp.where(column == zz, block, 0.0) for zz in range(ZZ)] + [jnp.zeros((8, 256), F32)]
        bd[128 * n:128 * n + 128, :] = jnp.concatenate(stack, axis=0).astype(BF16)

    eight = lax.broadcasted_iota(jnp.int32, (8, 128), 0)
    for k in range(NGX // 2):
        sides = []
        for dd in ((0,) + FAR)[2 * k:2 * k + 2]:
            if dd:
                acopies[dd].wait_recv()
            held = (arecv if dd else asend)[PLACES.index(dd)].astype(F32)
            value = decode(held) * held[48 + SHARE:48 + SHARE + 1, :]
            tails = []
            for t in range(2):
                a, b, c = (pltpu.roll(value[24 * t + 8 * n:24 * t + 8 * n + 8], 2 * n + 2, axis=0) for n in range(3))
                tails.append(jnp.where(eight < 2, a, jnp.where(eight < 4, b, c)))
            sides.append(jnp.concatenate([value] + tails, axis=0))
        high, rest = split(jnp.concatenate(sides, axis=1))
        product = jnp.dot(jnp.concatenate([high, rest], axis=0), bd[256 * k:256 * k + 256, :], preferred_element_type=F32)
        if k == 0:
            acc[...] = product
        else:
            acc[...] += product

    core = acc[0:80, :] + acc[80:160, :]
    for zz in range(ZZ):
        d2[80 * zz:80 * zz + 80, 0:RI] = core[:, RI * zz:RI * zz + RI]
    rows = jnp.concatenate([d2[pl.ds(c, ZL, stride=8), :][:, 0:RI] for c in range(SHARE)], axis=1)
    unit = scale_of(jnp.max(jnp.abs(rows), keepdims=True))
    words = encode(rows, 1.0 / unit)
    rest = [words[16 * k:16 * k + 16, 256:288] for k in range(3)] + [jnp.broadcast_to(unit, (16, 32))]
    csend[...] = jnp.concatenate([words[:, 0:128], words[:, 128:256], jnp.concatenate(rest, axis=1)], axis=0).astype(BF16)

    ccopies = []
    for dx, dh in ((2, 1), (1, 1), (3, 1), (0, 1), (2, 0), (1, 0), (3, 0)):
        k = 2 * dx + dh
        ccopies.append(pltpu.make_async_remote_copy(
            csend, theirs.at[4 * y_hi + quad], cs_sem.at[k], cr_sem.at[4 + 4 * y_hi + quad], device_id=charged(dx, dh), device_id_type=MESH))
    for dy, dc in ((1, 1), (1, 0), (0, 1)):
        ccopies.append(pltpu.make_async_remote_copy(
            csend, owns.at[quad], cs_sem.at[8 + 2 * dy + dc], cr_sem.at[quad], device_id=in_quad(dy, dc), device_id_type=MESH))
    for copy in ccopies:
        copy.start()
    for copy in xcopies + exchanges + list(acopies.values()):
        copy.wait_send()
    owns[quad] = csend[...]

    def opened(pieces, buf, at, low):
        rests = []
        for w in range(4):
            held = pieces[w].astype(F32)
            value = decode(held) * held[96:97, 96:97]
            for k in range(2):
                lanes = pl.ds(256 * w + 128 * k, 128)
                buf[pl.ds(at, ZL), lanes], buf[pl.ds(low, ZL), lanes] = split(value[ZL * k:ZL * k + ZL])
            rests.append(jnp.concatenate([value[96:112, 32 * k:32 * k + 32] for k in range(3)], axis=0))
        buf[pl.ds(at, ZL), 1024:1152], buf[pl.ds(low, ZL), 1024:1152] = split(jnp.concatenate(rests, axis=1))

    for dy, dc in ((0, 1), (1, 0), (1, 1)):
        w = quad_of(dy, dc)
        pltpu.make_async_copy(owns.at[w], owns.at[w], cr_sem.at[w]).wait()
    opened([owns[w] for w in range(4)], left_buf, 0, ZL)
    for near in range(2):
        b = rem(y_hi + near, 2)

        @pl.when(2 * quad + b != gz)
        def _():
            for w in range(4):
                k = 4 * b + w
                pltpu.make_async_copy(theirs.at[k], theirs.at[k], cr_sem.at[4 + k]).wait()

        @pl.when(2 * quad + b == gz)
        def _():
            for w in range(4):
                theirs[4 * b + w] = owns[w]

        at = pl.multiple_of(ZL * b, 16)
        opened([theirs[4 * b + w] for w in range(4)], right_buf, at, at + 128)
    right_buf[96:128, :] = jnp.zeros((32, 1152), BF16)
    right_buf[224:256, :] = jnp.zeros((32, 1152), BF16)
    gram = lax.dot_general(left_buf[...], right_buf[...], NT, preferred_element_type=F32)
    gram = (gram[0:ZL] + gram[ZL:2 * ZL]) * (1.0 / (RI * RJ * RP))
    gram = gram[:, 0:128] + gram[:, 128:256]
    unit = scale_of(jnp.max(jnp.abs(gram), keepdims=True))
    beyond = lax.broadcasted_iota(jnp.int32, (ZL, 128), 1) >= 96
    gsum[z_at] = jnp.where(beyond, unit, encode(gram, 1.0 / unit)).astype(BF16)

    gcopies = [
        pltpu.make_async_remote_copy(
            gsum.at[z_at], gsum.at[z_at], gs_sem.at[dz], gr_sem.at[z_at],
            device_id={"gx": y_lo * 8 + rem(z_at + dz, 8), "gz": gz, "gy": gy}, device_id_type=MESH)
        for dz in (4, 3, 5, 2, 6, 1, 7)
    ]
    for copy in gcopies:
        copy.start()
    for copy in ccopies:
        copy.wait_send()
    for dz in (7, 1, 6, 2, 5, 3, 4):
        w = rem(z_at + dz, 8)
        pltpu.make_async_copy(gsum.at[w], gsum.at[w], gr_sem.at[w]).wait()
    total = jnp.zeros((ZL, 128), F32)
    for k in range(8):
        held = gsum[k].astype(F32)
        total = total + decode(held) * held[:, 96:97]
    fin[quad] = total

    qcopies = [
        pltpu.make_async_remote_copy(
            fin.at[quad], fin.at[quad], qs_sem.at[2 * dy + dc], qr_sem.at[quad], device_id=in_quad(dy, dc), device_id_type=MESH)
        for dy, dc in ((1, 1), (1, 0), (0, 1))
    ]
    for copy in qcopies:
        copy.start()
    for copy in gcopies:
        copy.wait_send()
    for dy, dc in ((0, 1), (1, 0), (1, 1)):
        w = quad_of(dy, dc)
        pltpu.make_async_copy(fin.at[w], fin.at[w], qr_sem.at[w]).wait()
    out[...] = jnp.concatenate([fin[w][:, 0:96] for w in range(4)], axis=1)

    for copy in qcopies:
        copy.wait_send()


def body(field, x_factor, y_factor, species_basis_matrix):
    vmem = pl.BlockSpec(memory_space=pltpu.VMEM)
    dma = pltpu.SemaphoreType.DMA
    factors = (
        jnp.pad(y_factor.T.astype(F32), ((0, XL + 8), (0, 0)))
        + jnp.pad(x_factor.astype(F32), ((RJ, 8), (0, 128 - RI)))
        + jnp.pad(species_basis_matrix.T, ((RJ + XL, 8 - RP), (0, 128 - NS)))
    )
    return pl.pallas_call(
        kernel,
        out_shape=jax.ShapeDtypeStruct((ZL, NGZ * ZL), F32),
        in_specs=[pl.BlockSpec(memory_space=pltpu.HBM), vmem],
        out_specs=vmem,
        scratch_shapes=[
            pltpu.VMEM((NS, XL, ZL, 128), BF16),
            pltpu.VMEM((1024, 256), BF16),
            pltpu.VMEM((1024, 256), BF16),
            pltpu.VMEM((XL * ZL + ZL, 128), F32),
            pltpu.VMEM((XL * ZL + ZL, 128), F32),
            pltpu.VMEM((NGX, 64, 128), F32),
            pltpu.VMEM((NGX, 64, 128), BF16),
            pltpu.VMEM((NGX, 64, 128), BF16),
            pltpu.VMEM((16, 128), BF16),
            pltpu.VMEM((NGX, 16, 128), BF16),
            pltpu.VMEM((NGX * 128, 256), BF16),
            pltpu.VMEM((NGX, 64, 128), BF16),
            pltpu.VMEM((NGX, 64, 128), BF16),
            pltpu.VMEM((160, 256), F32),
            pltpu.VMEM((400, 128), F32),
            pltpu.VMEM((112, 128), BF16),
            pltpu.VMEM((4, 112, 128), BF16),
            pltpu.VMEM((8, 112, 128), BF16),
            pltpu.VMEM((96, 1152), BF16),
            pltpu.VMEM((256, 1152), BF16),
            pltpu.VMEM((8, ZL, 128), BF16),
            pltpu.VMEM((4, ZL, 128), F32),
            dma((CH,)), dma((CH,)), dma((CH,)), dma((NGX,)), dma((NGX,)), dma((NGX,)), dma((NGX,)),
            dma((12,)), dma((12,)), dma((8,)), dma((8,)), dma((4,)), dma((4,)),
        ],
        compiler_params=pltpu.CompilerParams(collective_id=0, has_side_effects=True, vmem_limit_bytes=53 * 1024 * 1024),
    )(field, factors)


def solution(mesh):
    placed = (P(None, "gx", "gz", "gy"), P("gx", None), P("gy", None), P())
    return jax.shard_map(body, mesh=mesh, in_specs=placed, out_specs=P("gz", None), check_vma=False)
```
